256 devices in a mesh: batch: 16 (over z, core), seq: 16 (over y, x).
Axes of the slice: x: 4, y: 4, z: 8, core: 2. Of those that a mesh axis runs over, the one named last changes fastest.
Arguments:
- tokens: bfloat16 [16, 16384, 1408], P('batch', 'seq'), may hold values from -24 to 24
- w_qkv: bfloat16 [1408, 4224], P(None, 'seq'), may hold values from -0.170450765 to 0.170450765
- vis_index: int32 [16, 2560], P('batch', 'seq'), may hold values from 0 to 1023, as said below
- counts: int32 [16, 16], P('batch'), may hold values from 96 to 160, as said below
- d_out: bfloat16 [16, 2560, 1408], P('batch', 'seq'), may hold values from -6 to 6
Outputs:
- attn_out: bfloat16 [16, 2560, 1408], P('batch', 'seq')
- d_tokens: bfloat16 [16, 16384, 1408], P('batch', 'seq')
- d_wqkv: float32 [1408, 4224], P(None, 'seq')
The draws below stay inside these ranges and needn't reach their ends.
Inputs may be any that keep to these rules, and one draw needn't show every extreme that they name: For every clip the 16 counts add up to exactly 2048, and some position block of every clip holds exactly 160. `vis_index`: within one position block's 160 entries all values differ; entry r names a visible tubelet when r is below that block's count and is ignored otherwise.
All inputs are finite; a program needn't handle non-finite values.
Results may differ from the reference program's by a relative error of at most 0.04.
Values may be sent and summed in bfloat16 or wider, within the bound.
A program may use at most 128 MiB of HBM per device.

```python
import math
import jax
import jax.numpy as jnp
from jax import lax

D = 1408
HEADS = 16
HEAD = 88
POS_DEV = 1024
VIS_DEV = 128
CAP = 160
CLIPS = 16
POSITIONS = 16384
SLOTS = 2560
N_SEQ = 16


def draw_tokens(key, part):
    noise = jnp.clip(jax.random.normal(jax.random.fold_in(key, 41), (CLIPS, POSITIONS, D), jnp.float32), -6.0, 6.0)
    rows = noise
    return rows.astype(jnp.bfloat16)


def draw_w_qkv(key, part):
    base_key = jax.random.fold_in(key, 51)
    base = jnp.clip(jax.random.normal(base_key, (D, 3 * D), jnp.float32), -6.0, 6.0) / math.sqrt(D)
    return base.astype(jnp.bfloat16)


def draw_counts(key, part):
    spread = VIS_DEV // 4
    shifts = jax.random.randint(jax.random.fold_in(key, 11), (CLIPS, N_SEQ // 2), 0, spread + 1)
    shifts = shifts.at[:, 0].set(spread)
    paired = jnp.stack([shifts, -shifts], axis=-1).reshape(CLIPS, N_SEQ)
    clip_keys = jax.random.split(jax.random.fold_in(key, 12), CLIPS)
    orders = jax.vmap(lambda single: jax.random.permutation(single, N_SEQ))(clip_keys)
    paired = jnp.take_along_axis(paired, orders, axis=1)
    return (VIS_DEV + paired).astype(jnp.int32)


def draw_vis_index(key, part):
    block_keys = jax.random.split(jax.random.fold_in(key, 21), CLIPS * N_SEQ)
    chosen = jax.vmap(lambda single: jax.random.permutation(single, POS_DEV)[:CAP])(block_keys)
    return chosen.reshape(CLIPS, N_SEQ * CAP).astype(jnp.int32)


def shard_levels(rng, extent, cuts, least, high):
    def one(dim, shards_of):
        draws = jax.random.uniform(jax.random.fold_in(jax.random.fold_in(rng, 6), dim), (shards_of,), jnp.float32, least / len(cuts), high / len(cuts))
        return jnp.repeat(jnp.exp(draws), extent[dim] // shards_of).reshape((-1,) + (1,) * (len(extent) - dim - 1))

    factor_of = one(*cuts[0])
    for cut in cuts[1:]:
        factor_of = factor_of * one(*cut)
    return factor_of


def normal_values(stream_key, dims, deviation, bound, cuts=(), held_as=jnp.bfloat16):
    result = deviation * jax.random.normal(stream_key, dims, jnp.float32)
    if cuts:
        result = result * shard_levels(stream_key, dims, cuts, -0.22, 0.18)
    return jnp.clip(result, -bound, bound).astype(held_as)


def setup_inputs(seed: int = 0) -> dict:
    splits = jax.random.split(jax.random.key(seed), 6)
    tokens = draw_tokens(jax.random.fold_in(splits[5], 71), 0)
    w_qkv = draw_w_qkv(jax.random.fold_in(splits[5], 71), 0)
    vis_index = draw_vis_index(jax.random.fold_in(splits[5], 71), 0)
    counts = draw_counts(jax.random.fold_in(splits[5], 71), 0)
    d_out = normal_values(splits[4], (CLIPS, SLOTS, D), 1.0, 6.0, ((0, 16), (1, 16)))
    return dict(tokens=tokens, w_qkv=w_qkv, vis_index=vis_index, counts=counts, d_out=d_out)


EPSILON = 1e-06

def layout(index_row, count_row):
    visible = VIS_DEV * N_SEQ
    inclusive = jnp.cumsum(count_row).astype(jnp.int32)
    exclusive = (inclusive - count_row).astype(jnp.int32)
    ordinal = jnp.arange(visible, dtype=jnp.int32)
    owner = lax.optimization_barrier(jnp.sum((ordinal[:, None] >= inclusive[None, :]).astype(jnp.int32), axis=1)).astype(jnp.int32)
    within = (ordinal - jnp.take(exclusive, owner)).astype(jnp.int32)
    slot_index = (owner * CAP + within).astype(jnp.int32)
    positions = (owner * POS_DEV + jnp.take(index_row, slot_index)).astype(jnp.int32)
    return (slot_index, positions)

def one_head(queries, key_rows, values, gradient):
    inv_scale = HEAD ** (-0.5)
    scores = jnp.dot(queries, key_rows.T, preferred_element_type=jnp.float32) * inv_scale
    row_peak = lax.optimization_barrier(jnp.max(scores, axis=1, keepdims=True))
    weights = jnp.exp(scores - row_peak)
    probs = weights / lax.optimization_barrier(jnp.sum(weights, axis=1, keepdims=True))
    probs_low = probs.astype(jnp.bfloat16)
    attended = jnp.dot(probs_low, values, preferred_element_type=jnp.float32).astype(jnp.bfloat16)
    d_probs = jnp.dot(gradient, values.T, preferred_element_type=jnp.float32)
    row_delta = lax.optimization_barrier(jnp.sum(gradient.astype(jnp.float32) * attended.astype(jnp.float32), axis=1, keepdims=True))
    d_scores = (probs * (d_probs - row_delta) * inv_scale).astype(jnp.bfloat16)
    d_query = jnp.dot(d_scores, key_rows, preferred_element_type=jnp.float32).astype(jnp.bfloat16)
    d_key = jnp.dot(d_scores.T, queries, preferred_element_type=jnp.float32).astype(jnp.bfloat16)
    d_value = jnp.dot(probs_low.T, gradient, preferred_element_type=jnp.float32).astype(jnp.bfloat16)
    return (attended, jnp.stack([d_query, d_key, d_value]))

def one_clip(inputs, w_qkv):
    clip_tokens, index_row, count_row, clip_grad = inputs
    slot_index, positions = layout(index_row, count_row)
    picked = jnp.take(clip_tokens, positions, axis=0).astype(jnp.float32)
    centred = picked - lax.optimization_barrier(jnp.mean(picked, axis=1, keepdims=True))
    inv_std = lax.rsqrt(lax.optimization_barrier(jnp.mean(centred * centred, axis=1, keepdims=True)) + EPSILON)
    normed = centred * inv_std
    normed_low = normed.astype(jnp.bfloat16)
    visible = normed.shape[0]
    projected = jnp.dot(normed_low, w_qkv, preferred_element_type=jnp.float32).astype(jnp.bfloat16)
    projected = projected.reshape(visible, HEADS, 3, HEAD).transpose(1, 2, 0, 3)
    grad_rows = jnp.take(clip_grad, slot_index, axis=0).reshape(visible, HEADS, HEAD).transpose(1, 0, 2)
    attended, d_parts = lax.map(lambda group: one_head(*group), (projected[:, 0], projected[:, 1], projected[:, 2], grad_rows))
    attended = attended.transpose(1, 0, 2).reshape(visible, D)
    clip_out = jnp.zeros((SLOTS, D), jnp.bfloat16).at[slot_index].set(attended)
    d_projected = d_parts.transpose(2, 0, 1, 3).reshape(visible, 3 * D)
    d_weight = jnp.dot(normed_low.T, d_projected, preferred_element_type=jnp.float32)
    d_normed = jnp.dot(d_projected, w_qkv.T, preferred_element_type=jnp.float32)
    d_picked = inv_std * (d_normed - lax.optimization_barrier(jnp.mean(d_normed, axis=1, keepdims=True)) - normed * lax.optimization_barrier(jnp.mean(d_normed * normed, axis=1, keepdims=True)))
    clip_dtok = jnp.zeros((POSITIONS, D), jnp.float32).at[positions].set(d_picked).astype(jnp.bfloat16)
    return (clip_out, clip_dtok, d_weight)

def reference(tokens, w_qkv, vis_index, counts, d_out):

    def clip_step(running, inputs):
        clip_out, clip_dtok, d_weight = one_clip(inputs, w_qkv)
        return (running + d_weight, (clip_out, clip_dtok))
    initial = jnp.zeros((D, 3 * D), jnp.float32)
    d_wqkv, (attn_out, d_tokens) = lax.scan(clip_step, initial, (tokens, vis_index, counts, d_out))
    return (attn_out, d_tokens, d_wqkv)
```

```python
import jax
import jax.numpy as jnp
from jax import lax
from jax.experimental import pallas as pl
from jax.experimental.pallas import tpu as pltpu
from jax.sharding import PartitionSpec as P

D = 1408
HEAD = 88
HEADS = 16
CAP = 160
HALF = 80
SURE = 96
TAIL = CAP - SURE
LIVE = 2048
PACKED = LIVE - HEADS * SURE
LANES = 128
WIDE = 3 * LANES
SEQ = 16
SIDE = 4
DEPTH = 8
EPSILON = 1e-06
LOG2E = 1.4426950408889634
LN2 = 0.6931471805599453
SCALE = HEAD ** (-0.5)
MESH = pl.DeviceIdType.MESH
BF = jnp.bfloat16
F32 = jnp.float32
VMEM = pltpu.VMEM
VMEM_BYTES = 60 * 2**20


def dot(left, right, left_dim=1, right_dim=0):
    return lax.dot_general(
        left, right, (((left_dim,), (right_dim,)), ((), ())), preferred_element_type=F32
    )


def wrap(value, size):
    return lax.rem(value + 2 * size, size)


PART = {0: (0, 80), 1: (0, 48), -1: (48, 32)}
BLOCK = {"o": (0, 0), "m": (-1, 0), "p": (1, 0), "a": (2, 1), "b": (2, -1)}
KEYS = (
    [("P1", s) for s in (1, -1)]
    + [("P1f", s) for s in (1, -1)]
    + [("P2", j, s) for j in "ompab" for s in (1, -1)]
    + [("P2f", j, s) for j in "omp" for s in (1, -1)]
    + [("P2f", "a", 1), ("P2f", "b", -1)]
)
IDS = {key: at for at, key in enumerate(KEYS)}


class Tree:
    def __init__(self, me, way, blocks, send_sem, recv_sem):
        self.y, self.x, self.way = me // SIDE, lax.rem(me, SIDE), way
        self.blocks, self.send_sem, self.recv_sem = blocks, send_sem, recv_sem
        self.memo = {}

    def node(self, half, first, second):
        key = (half, first % SIDE, second % SIDE)
        if key not in self.memo:
            first, second = first * self.way, second * self.way
            dy, dx = (second, first) if half == 0 else (first, second)
            self.memo[key] = wrap(self.y + dy, SIDE) * SIDE + wrap(self.x + dx, SIDE)
        return self.memo[key]

    def describe(self, key):
        kind, sign = key[0], key[-1]
        if kind == "P1":
            return (0, 0), 0, 0, sign
        if kind == "P1f":
            return (-sign, 0), sign, 0, sign
        first, part = BLOCK[key[1]]
        if kind == "P2":
            return (first, 0), part, 1, sign
        return (first, -sign), sign, 1, sign

    def copy(self, half, key, receiver=False):
        (first, second), part, axis, sign = self.describe(key)
        if receiver:
            first, second = (first - sign, second) if axis == 0 else (first, second - sign)
        start, rows = PART[part]
        ref = self.blocks.at[self.node(half, first, second), pl.ds(half * HALF + start, rows)]
        to = self.node(half, sign, 0) if axis == 0 else self.node(half, 0, sign)
        return pltpu.make_async_remote_copy(
            src_ref=ref, dst_ref=ref,
            send_sem=self.send_sem.at[half, IDS[key]], recv_sem=self.recv_sem.at[half, IDS[key]],
            device_id={"seq": to}, device_id_type=MESH,
        )

    def start(self, *key):
        for half in (0, 1):
            self.copy(half, key).start()

    def arrive(self, *key):
        for half in (0, 1):
            self.copy(half, key, True).wait_recv()

    def first(self):
        for s in (1, -1):
            self.start("P1", s)
        for s in (1, -1):
            self.start("P2", "o", s)

    def rest(self, done):
        for s in (1, -1):
            self.arrive("P1", s)
            self.start("P1f", s)
        for s in (1, -1):
            self.start("P2", "m", s)
            self.start("P2", "p", s)
        done([(-1, 0), (1, 0)])
        for s in (1, -1):
            self.arrive("P2", "o", s)
            self.start("P2f", "o", s)
        for s in (1, -1):
            self.arrive("P1f", s)
            for t in (1, -1):
                self.start("P2", "a" if s == 1 else "b", t)
        done([(0, -1), (0, 1), (2, 0)])
        for j in ("m", "p"):
            for s in (1, -1):
                self.arrive("P2", j, s)
                self.start("P2f", j, s)
        done([(-1, -1), (-1, 1), (1, -1), (1, 1)])
        for j in ("a", "b"):
            for s in (1, -1):
                self.arrive("P2", j, s)
                if ("P2f", j, s) in IDS:
                    self.start("P2f", j, s)
        for s in (1, -1):
            self.arrive("P2f", "o", s)
        done([(2, -1), (2, 1), (0, 2)])
        for j in ("m", "p"):
            for s in (1, -1):
                self.arrive("P2f", j, s)
        self.arrive("P2f", "a", 1)
        self.arrive("P2f", "b", -1)
        done([(-1, 2), (1, 2), (2, 2)])

    def finish(self):
        for key in KEYS:
            for half in (0, 1):
                self.copy(half, key).wait_send()


def gather_kernel(
    tokens, index, w, d_out,
    everyone_out, qkv, g, normed_out, inv_out, w_rows,
    everyone, w3, g_send, ring_send, ring_recv, g_ssem, g_rsem, out_sem,
):
    me = lax.axis_index("seq")
    core = lax.rem(lax.axis_index("batch"), 2)
    barrier = pltpu.get_barrier_semaphore()
    for step in range(1, SEQ):
        pl.semaphore_signal(
            barrier, inc=1, device_id={"seq": lax.rem(me + step, SEQ)}, device_id_type=MESH
        )

    hot = (lax.broadcasted_iota(jnp.int32, (tokens.shape[1], CAP), 0) == index[...]).astype(BF)
    picked = dot(hot, tokens[0], 0, 0)
    centred = picked - jnp.mean(picked, axis=1, keepdims=True)
    inv_std = lax.rsqrt(jnp.mean(centred * centred, axis=1, keepdims=True) + EPSILON)
    normed = centred * inv_std
    everyone[me] = normed.astype(BF)
    pl.semaphore_wait(barrier, SEQ - 1)
    tree = Tree(me, 1 - 2 * core, everyone, ring_send, ring_recv)
    tree.first()

    normed_out[...] = normed
    inv_out[...] = jnp.broadcast_to(inv_std, inv_out.shape)
    g_send[...] = jnp.zeros_like(g_send)
    for head in range(HEADS):
        g_send[head, :, :HEAD] = d_out[0, :, head * HEAD:(head + 1) * HEAD]

    def g_copy(step):
        to = lax.rem(me + step, SEQ)
        return pltpu.make_async_remote_copy(
            src_ref=g_send.at[to], dst_ref=g.at[me],
            send_sem=g_ssem.at[step], recv_sem=g_rsem.at[step],
            device_id={"seq": to}, device_id_type=MESH,
        )

    def g_arrival(step):
        origin = lax.rem(me - step + SEQ, SEQ)
        return pltpu.make_async_remote_copy(
            src_ref=g_send.at[origin], dst_ref=g.at[origin],
            send_sem=g_ssem.at[step], recv_sem=g_rsem.at[step],
            device_id={"seq": origin}, device_id_type=MESH,
        )

    def g_start(step, carry):
        g_copy(step).start()
        return carry

    w3[...] = jnp.zeros_like(w3)
    for part in range(3):
        w3[:, part * LANES:part * LANES + HEAD] = w[:, part * HEAD:(part + 1) * HEAD]

    lane = lax.broadcasted_iota(jnp.int32, (1, WIDE), 1)
    column_scale = jnp.where(lane < LANES, SCALE * LOG2E, 1.0).astype(F32)

    def project(places):
        rows = [everyone[owner, pl.ds(HALF * half, HALF), :] for owner, half in places]
        result = (dot(jnp.concatenate(rows, axis=0), w3[...]) * column_scale).astype(BF)
        for at, (owner, half) in enumerate(places):
            qkv[owner, pl.ds(HALF * half, HALF), :] = result[at * HALF:(at + 1) * HALF]
            part = (owner, pl.ds(HALF * half, HALF))
            pltpu.make_async_copy(everyone.at[part], everyone_out.at[part], out_sem).start()

    def done(offsets):
        project([(tree.node(half, *offset), half) for half in (0, 1) for offset in offsets])

    done([(0, 0)])
    tree.rest(done)
    lax.fori_loop(1, SEQ, g_start, 0)
    g[me] = g_send[me]
    for part in range(3):
        w_rows[part] = w3[:, part * LANES:(part + 1) * LANES].T[:SURE]

    def g_wait(step, carry):
        g_copy(step).wait_send()
        g_arrival(step).wait_recv()
        return carry

    lax.fori_loop(1, SEQ, g_wait, 0)
    tree.finish()
    pltpu.make_async_copy(everyone, everyone_out, out_sem).wait()


def gather_call(tokens, index, w, d_out):
    vmem = pl.BlockSpec(memory_space=VMEM)
    return pl.pallas_call(
        gather_kernel,
        out_shape=(
            jax.ShapeDtypeStruct((SEQ, CAP, D), BF),
            jax.ShapeDtypeStruct((SEQ, CAP, WIDE), BF),
            jax.ShapeDtypeStruct((SEQ, CAP, LANES), BF),
            jax.ShapeDtypeStruct((CAP, D), F32),
            jax.ShapeDtypeStruct((CAP, LANES), F32),
            jax.ShapeDtypeStruct((3, SURE, D), BF),
        ),
        in_specs=[vmem] * 4,
        out_specs=(pl.BlockSpec(memory_space=pl.ANY),) + (vmem,) * 5,
        scratch_shapes=[
            VMEM((SEQ, CAP, D), BF),
            VMEM((D, WIDE), BF),
            VMEM((HEADS, CAP, LANES), BF),
            pltpu.SemaphoreType.DMA((2, len(KEYS))),
            pltpu.SemaphoreType.DMA((2, len(KEYS))),
            pltpu.SemaphoreType.DMA((SEQ,)),
            pltpu.SemaphoreType.DMA((SEQ,)),
            pltpu.SemaphoreType.DMA,
        ],
        compiler_params=pltpu.CompilerParams(
            collective_id=1, has_side_effects=True, vmem_limit_bytes=VMEM_BYTES
        ),
        name="gather_project",
    )(tokens, index, w, d_out)


QB = 256


def attend(q, kt, k, va, vat, g, att, dq, dkt, dvt, between):
    dkt[...] = jnp.zeros_like(dkt)
    dvt[...] = jnp.zeros_like(dvt)
    lane = lax.broadcasted_iota(jnp.int32, (QB, LANES), 1)

    def block(at, carry):
        between(at)
        rows = pl.ds(at * QB, QB)
        queries = q[rows]
        scores = dot(queries, kt[...])
        weights = jnp.exp2(scores - jnp.max(scores, axis=1, keepdims=True)).astype(BF)
        raw = dot(weights, va[...])
        inverse = 1.0 / raw[:, HEAD:HEAD + 1]
        out = jnp.where(lane < HEAD, raw * inverse, 0.0)
        att[rows] = out.astype(BF)
        scaled = (g[rows].astype(F32) * inverse).astype(BF)
        delta = jnp.sum(scaled.astype(F32) * out, axis=1, keepdims=True)
        high = delta.astype(BF).astype(F32)
        extended = jnp.where(lane == HEAD, -high, scaled.astype(F32))
        extended = jnp.where(lane == HEAD + 1, high - delta, extended).astype(BF)
        d_scores = weights * dot(extended, vat[...]).astype(BF)
        dq[rows] = (dot(d_scores, k[...]) * SCALE).astype(BF)
        dkt[...] += dot(queries, d_scores, 0, 0)
        dvt[...] += dot(scaled, weights, 0, 0)
        return carry

    lax.fori_loop(0, LIVE // QB, block, 0)


HALF_LANES = 768
SHARD = WIDE // DEPTH


def attend_kernel(
    everyone_in, qkv, g_in, rank, normed_in, inv_in, w_rows, index,
    attn_out, d_tokens, d_wqkv,
    everyone, q, k, v, g, kt, vt, att, dq, dkt, dvt,
    w_side, d_slots, att_send, att_recv, d_recv, part_send, part_recv,
    dwt, pair_send, pair_recv, z_send, z_recv, z_all, z_other,
    w_ssem, w_rsem, d_ssem, d_rsem, p_ssem, p_rsem, a_ssem, a_rsem, c_ssem, c_rsem, z_ssem, z_rsem,
    in_sem,
):
    me = lax.axis_index("seq")
    batch = lax.axis_index("batch")
    core, z = lax.rem(batch, 2), batch // 2
    y, x = me // SIDE, lax.rem(me, SIDE)
    place = (y, x)

    def peer(axis, step):
        if axis == 0:
            return wrap(y + step, SIDE) * SIDE + x
        return y * SIDE + wrap(x + step, SIDE)

    def above(step):
        return wrap(z + step, DEPTH) * 2 + core

    other = batch + 1 - 2 * core
    barrier = pltpu.get_barrier_semaphore()
    for step in range(1, SEQ):
        pl.semaphore_signal(
            barrier, inc=1, device_id={"seq": lax.rem(me + step, SEQ)}, device_id_type=MESH
        )
    for step in range(1, DEPTH):
        pl.semaphore_signal(
            barrier, inc=1, device_id={"batch": above(step)}, device_id_type=MESH
        )
    pl.semaphore_signal(barrier, inc=1, device_id={"batch": other}, device_id_type=MESH)

    fetch = pltpu.make_async_copy(everyone_in, everyone, in_sem)
    fetch.start()

    def w_own(axis, sign):
        return pltpu.make_async_remote_copy(
            src_ref=w_rows, dst_ref=w_side.at[axis, place[axis], :, pl.ds(0, SURE)],
            send_sem=w_ssem.at[axis, (1 - sign) // 2], recv_sem=w_rsem.at[axis, (1 - sign) // 2],
            device_id={"seq": peer(axis, sign)}, device_id_type=MESH,
        )

    def w_from(axis, sign):
        ref = w_side.at[axis, wrap(place[axis] - sign, SIDE), :, pl.ds(0, SURE)]
        return pltpu.make_async_remote_copy(
            src_ref=w_rows, dst_ref=ref,
            send_sem=w_ssem.at[axis, (1 - sign) // 2], recv_sem=w_rsem.at[axis, (1 - sign) // 2],
            device_id={"seq": peer(axis, -sign)}, device_id_type=MESH,
        )

    def w_onward(axis, sign, receiver=False):
        origin = wrap(place[axis] - (2 * sign if receiver else sign), SIDE)
        slot = 2 + (1 - sign) // 2
        ref = w_side.at[axis, origin, :, pl.ds(0 if sign == 1 else SURE // 2, SURE // 2)]
        return pltpu.make_async_remote_copy(
            src_ref=ref, dst_ref=ref,
            send_sem=w_ssem.at[axis, slot], recv_sem=w_rsem.at[axis, slot],
            device_id={"seq": peer(axis, sign)}, device_id_type=MESH,
        )

    pl.semaphore_wait(barrier, SEQ - 1 + DEPTH)
    for axis in (0, 1):
        for sign in (1, -1):
            w_own(axis, sign).start()

    hot = (lax.broadcasted_iota(jnp.int32, (PACKED, HEADS * TAIL), 0) == rank[...]).astype(BF)
    sure_rows = HEADS * SURE
    tail = dot(hot, qkv[:, SURE:, :].reshape(HEADS * TAIL, WIDE)).astype(BF)
    for part, ref in enumerate((q, k, v)):
        lanes = slice(part * LANES, (part + 1) * LANES)
        ref[:sure_rows] = qkv[:, :SURE, lanes].reshape(sure_rows, LANES)
        ref[sure_rows:] = tail[:, lanes]
    g[:sure_rows] = g_in[:, :SURE, :].reshape(sure_rows, LANES)
    g[sure_rows:] = dot(hot, g_in[:, SURE:, :].reshape(HEADS * TAIL, LANES)).astype(BF)
    lane = lax.broadcasted_iota(jnp.int32, (LIVE, LANES), 1)
    ones = (lane == HEAD) | (lane == HEAD + 1)
    v[...] = jnp.where(ones, 1.0, v[...].astype(F32)).astype(BF)
    kt[...] = k[...].T
    vt[...] = v[...].T

    w_side[:, :, :, SURE:, :] = jnp.zeros((2, SIDE, 3, LANES - SURE, D), BF)
    for axis in (0, 1):
        w_side[axis, place[axis], :, :SURE, :] = w_rows[...]

    def between(at):
        @pl.when(at == 4)
        def _():
            for axis in (0, 1):
                for sign in (1, -1):
                    w_from(axis, sign).wait_recv()
                    w_onward(axis, sign).start()

    attend(q, kt, k, v, vt, g, att, dq, dkt, dvt, between)

    dk = (dkt[...].T * LN2).astype(BF)
    dv = dvt[...].T.astype(BF)
    packed = jnp.concatenate(
        [dq[sure_rows:], dk[sure_rows:], dv[sure_rows:], att[sure_rows:]], axis=1
    )
    loose = dot(hot, packed, 0, 0).astype(BF).reshape(SIDE, SIDE, TAIL, 4 * LANES)
    for part, value in enumerate((dq[:sure_rows], dk[:sure_rows], dv[:sure_rows])):
        lanes = slice(part * LANES, (part + 1) * LANES)
        d_slots[:, :, :SURE, lanes] = value.reshape(SIDE, SIDE, SURE, LANES)
    d_slots[:, :, SURE:, :] = loose[..., :WIDE]
    att_send[:, :, :SURE, :] = att[:sure_rows].reshape(SIDE, SIDE, SURE, LANES)
    att_send[:, :, SURE:, :] = loose[..., WIDE:]

    def d_copy(axis, step):
        to = wrap(place[axis] + step, SIDE)
        if axis == 0:
            src = d_slots.at[to, :, pl.ds(0, HALF)]
        else:
            src = d_slots.at[:, to, pl.ds(HALF, HALF)]
        return pltpu.make_async_remote_copy(
            src_ref=src, dst_ref=d_recv.at[axis, place[axis]],
            send_sem=d_ssem.at[axis, step], recv_sem=d_rsem.at[axis, step],
            device_id={"seq": peer(axis, step)}, device_id_type=MESH,
        )

    def d_arrival(axis, step):
        ref = d_recv.at[axis, wrap(place[axis] - step, SIDE)]
        return pltpu.make_async_remote_copy(
            src_ref=ref, dst_ref=ref,
            send_sem=d_ssem.at[axis, step], recv_sem=d_rsem.at[axis, step],
            device_id={"seq": peer(axis, step)}, device_id_type=MESH,
        )

    for step in (2, 1, 3):
        for axis in (0, 1):
            d_copy(axis, step).start()
    d_recv[0, y] = d_slots[y, :, :HALF, :]
    d_recv[1, x] = d_slots[:, x, HALF:, :]

    def a_copy(step):
        to = lax.rem(me + step, SEQ)
        return pltpu.make_async_remote_copy(
            src_ref=att_send.at[to // SIDE, lax.rem(to, SIDE)], dst_ref=att_recv.at[me],
            send_sem=a_ssem.at[step], recv_sem=a_rsem.at[step],
            device_id={"seq": to}, device_id_type=MESH,
        )

    def a_arrival(step):
        ref = att_recv.at[lax.rem(me - step + SEQ, SEQ)]
        return pltpu.make_async_remote_copy(
            src_ref=ref, dst_ref=ref,
            send_sem=a_ssem.at[step], recv_sem=a_rsem.at[step],
            device_id={"seq": lax.rem(me - step + SEQ, SEQ)}, device_id_type=MESH,
        )

    def a_start(step, carry):
        a_copy(step).start()
        return carry

    lax.fori_loop(1, SEQ, a_start, 0)
    att_recv[me] = att_send[y, x]

    fetch.wait()
    for first, last in ((0, 512), (512, 1024), (1024, D)):
        dwt[:, first:last] = dot(
            d_slots[...].reshape(SEQ * CAP, WIDE),
            everyone[:, :, first:last].reshape(SEQ * CAP, last - first), 0, 0,
        )

    def lanes_of(which):
        return pl.ds(pl.multiple_of(which * (D - HALF_LANES), LANES), HALF_LANES)

    pair_send[...] = dwt[:, lanes_of(1 - core)].astype(BF)

    def c_copy(slot, src, dst):
        return pltpu.make_async_remote_copy(
            src_ref=src, dst_ref=dst, send_sem=c_ssem.at[slot], recv_sem=c_rsem.at[slot],
            device_id={"batch": other}, device_id_type=MESH,
        )

    pair_copy = c_copy(0, pair_send, pair_recv)
    pair_copy.start()

    def p_copy(axis, step):
        return pltpu.make_async_remote_copy(
            src_ref=part_send.at[axis, wrap(place[axis] + step, SIDE)],
            dst_ref=part_recv.at[axis, place[axis]],
            send_sem=p_ssem.at[axis, step], recv_sem=p_rsem.at[axis, step],
            device_id={"seq": peer(axis, step)}, device_id_type=MESH,
        )

    def p_arrival(axis, step):
        ref = part_recv.at[axis, wrap(place[axis] - step, SIDE)]
        return pltpu.make_async_remote_copy(
            src_ref=ref, dst_ref=ref,
            send_sem=p_ssem.at[axis, step], recv_sem=p_rsem.at[axis, step],
            device_id={"seq": peer(axis, step)}, device_id_type=MESH,
        )

    for axis in (0, 1):
        for sign in (1, -1):
            w_onward(axis, sign, True).wait_recv()
    for axis in (0, 1):
        for step in (1, 2, 3):
            d_arrival(axis, step).wait_recv()
        left = jnp.concatenate(
            [d_recv[axis, head].reshape(SIDE * HALF, WIDE) for head in range(SIDE)], axis=1
        )
        partial = dot(left, w_side[axis].reshape(SIDE * WIDE, D))
        part_send[1 - axis] = partial.astype(BF).reshape(SIDE, HALF, D)
        for step in (2, 1, 3):
            p_copy(1 - axis, step).start()
    for axis in (0, 1):
        part_recv[axis, place[axis]] = part_send[axis, place[axis]]

    pair_copy.wait()
    z_send[...] = (dwt[:, lanes_of(core)] + pair_recv[...].astype(F32)).astype(BF).reshape(
        DEPTH, SHARD, HALF_LANES
    )

    def z_copy(phase, step):
        to = wrap(z + step, DEPTH)
        return pltpu.make_async_remote_copy(
            src_ref=z_send.at[to] if phase == 0 else z_all.at[z],
            dst_ref=z_recv.at[z] if phase == 0 else z_all.at[z],
            send_sem=z_ssem.at[phase, step], recv_sem=z_rsem.at[phase, step],
            device_id={"batch": above(step)}, device_id_type=MESH,
        )

    def z_arrival(phase, step):
        ref = (z_recv if phase == 0 else z_all).at[wrap(z - step, DEPTH)]
        return pltpu.make_async_remote_copy(
            src_ref=ref, dst_ref=ref,
            send_sem=z_ssem.at[phase, step], recv_sem=z_rsem.at[phase, step],
            device_id={"batch": above(step)}, device_id_type=MESH,
        )

    for step in (4, 3, 5, 2, 6, 1, 7):
        z_copy(0, step).start()
    z_recv[z] = z_send[z]

    def a_wait(step, carry):
        a_copy(step).wait_send()
        a_arrival(step).wait_recv()
        return carry

    lax.fori_loop(1, SEQ, a_wait, 0)
    for head in range(HEADS):
        attn_out[0, :, head * HEAD:(head + 1) * HEAD] = att_recv[head, :, :HEAD]

    for step in range(1, DEPTH):
        z_arrival(0, step).wait_recv()
    total = z_recv[0].astype(F32)
    for at in range(1, DEPTH):
        total = total + z_recv[at].astype(F32)
    z_all[z] = total.astype(BF)
    for step in (4, 3, 5, 2, 6, 1, 7):
        z_copy(1, step).start()

    for axis in (0, 1):
        for step in (1, 2, 3):
            p_arrival(axis, step).wait_recv()
    halves = []
    for axis in (1, 0):
        value = part_recv[axis, 0].astype(F32)
        for at in range(1, SIDE):
            value = value + part_recv[axis, at].astype(F32)
        halves.append(value)
    d_normed = jnp.concatenate(halves, axis=0)
    normed = normed_in[...]
    d_picked = inv_in[:, :1] * (
        d_normed
        - jnp.mean(d_normed, axis=1, keepdims=True)
        - normed * jnp.mean(d_normed * normed, axis=1, keepdims=True)
    )
    spread = (lax.broadcasted_iota(jnp.int32, (d_tokens.shape[1], CAP), 0) == index[...]).astype(BF)
    d_tokens[0] = dot(spread, d_picked.astype(BF)).astype(BF)

    for step in range(1, DEPTH):
        z_arrival(1, step).wait_recv()
    last = c_copy(1, z_all, z_other)
    last.start()
    last.wait()
    mine, theirs = (
        ref[...].astype(F32).reshape(WIDE, HALF_LANES) for ref in (z_all, z_other)
    )
    low = jnp.where(core == 0, mine, theirs)
    high = jnp.where(core == 0, theirs, mine)
    overlap = 2 * HALF_LANES - D
    full = jnp.concatenate([low, high[:, overlap:]], axis=1)
    for part in range(3):
        d_wqkv[:, part * HEAD:(part + 1) * HEAD] = full[part * LANES:(part + 1) * LANES].T[:, :HEAD]

    for axis in (0, 1):
        for sign in (1, -1):
            w_own(axis, sign).wait_send()
            w_onward(axis, sign).wait_send()
        for step in (1, 2, 3):
            d_copy(axis, step).wait_send()
            p_copy(axis, step).wait_send()
    for step in range(1, DEPTH):
        z_copy(0, step).wait_send()
        z_copy(1, step).wait_send()


def attend_call(everyone, qkv, g, rank, normed, inv, w_rows, index, positions):
    vmem = pl.BlockSpec(memory_space=VMEM)
    dma = pltpu.SemaphoreType.DMA
    return pl.pallas_call(
        attend_kernel,
        out_shape=(
            jax.ShapeDtypeStruct((1, CAP, D), BF),
            jax.ShapeDtypeStruct((1, positions, D), BF),
            jax.ShapeDtypeStruct((D, 3 * HEAD), F32),
        ),
        in_specs=[pl.BlockSpec(memory_space=pl.ANY)] + [vmem] * 7,
        out_specs=(vmem,) * 3,
        scratch_shapes=[
            VMEM((SEQ, CAP, D), BF),
            VMEM((LIVE, LANES), BF),
            VMEM((LIVE, LANES), BF),
            VMEM((LIVE, LANES), BF),
            VMEM((LIVE, LANES), BF),
            VMEM((LANES, LIVE), BF),
            VMEM((LANES, LIVE), BF),
            VMEM((LIVE, LANES), BF),
            VMEM((LIVE, LANES), BF),
            VMEM((LANES, LIVE), F32),
            VMEM((LANES, LIVE), F32),
            VMEM((2, SIDE, 3, LANES, D), BF),
            VMEM((SIDE, SIDE, CAP, WIDE), BF),
            VMEM((SIDE, SIDE, CAP, LANES), BF),
            VMEM((SEQ, CAP, LANES), BF),
            VMEM((2, SIDE, SIDE, HALF, WIDE), BF),
            VMEM((2, SIDE, HALF, D), BF),
            VMEM((2, SIDE, HALF, D), BF),
            VMEM((WIDE, D), F32),
            VMEM((WIDE, HALF_LANES), BF),
            VMEM((WIDE, HALF_LANES), BF),
            VMEM((DEPTH, SHARD, HALF_LANES), BF),
            VMEM((DEPTH, SHARD, HALF_LANES), BF),
            VMEM((DEPTH, SHARD, HALF_LANES), BF),
            VMEM((DEPTH, SHARD, HALF_LANES), BF),
            dma((2, 4)), dma((2, 4)),
            dma((2, 4)), dma((2, 4)),
            dma((2, 4)), dma((2, 4)),
            dma((SEQ,)), dma((SEQ,)),
            dma((2,)), dma((2,)),
            dma((2, DEPTH)), dma((2, DEPTH)),
            dma,
        ],
        compiler_params=pltpu.CompilerParams(
            collective_id=2, has_side_effects=True, vmem_limit_bytes=VMEM_BYTES
        ),
        name="attend_backward",
    )(everyone, qkv, g, rank, normed, inv, w_rows, index)


def per_device(tokens, w_qkv, vis_index, counts, d_out):
    extra = counts[0] - SURE
    order = jnp.arange(SEQ, dtype=jnp.int32)
    before = jnp.sum(jnp.where(order[None, :] < order[:, None], extra[None, :], 0), axis=1)
    within = jnp.arange(TAIL, dtype=jnp.int32)
    rank = jnp.where(within[None, :] < extra[:, None], before[:, None] + within[None, :], -1)
    rank = rank.reshape(1, SEQ * TAIL).astype(jnp.int32)
    everyone, qkv, g, normed, inv, w_rows = gather_call(tokens, vis_index, w_qkv, d_out)
    return tuple(
        attend_call(everyone, qkv, g, rank, normed, inv, w_rows, vis_index, tokens.shape[1])
    )


def solution(mesh):
    placed = (
        P("batch", "seq", None),
        P(None, "seq"),
        P("batch", "seq"),
        P("batch", None),
        P("batch", "seq", None),
    )
    return jax.shard_map(
        per_device,
        mesh=mesh,
        in_specs=placed,
        out_specs=(P("batch", "seq", None), P("batch", "seq", None), P(None, "seq")),
        check_vma=False,
    )
```

```python
import jax
import jax.numpy as jnp
from jax import lax
from jax.experimental import pallas as pl
from jax.experimental.pallas import tpu as pltpu
from jax.sharding import PartitionSpec as P

D = 1408
HEAD = 88
HEADS = 16
CAP = 160
HALF = 80
SURE = 96
TAIL = CAP - SURE
LIVE = 2048
PACKED = LIVE - HEADS * SURE
LANES = 128
WIDE = 3 * LANES
SEQ = 16
SIDE = 4
DEPTH = 8
EPSILON = 1e-06
LOG2E = 1.4426950408889634
LN2 = 0.6931471805599453
SCALE = HEAD ** (-0.5)
MESH = pl.DeviceIdType.MESH
BF = jnp.bfloat16
F32 = jnp.float32
VMEM = pltpu.VMEM
VMEM_BYTES = 62 * 2**20


def dot(left, right, left_dim=1, right_dim=0):
    return lax.dot_general(
        left, right, (((left_dim,), (right_dim,)), ((), ())), preferred_element_type=F32
    )


def wrap(value, size):
    return lax.rem(value + 2 * size, size)


PART = {0: (0, 80), 1: (0, 48), -1: (48, 32)}
BLOCK = {"o": (0, 0), "m": (-1, 0), "p": (1, 0), "a": (2, 1), "b": (2, -1)}
KEYS = (
    [("P1", s) for s in (1, -1)]
    + [("P1f", s) for s in (1, -1)]
    + [("P2", j, s) for j in "ompab" for s in (1, -1)]
    + [("P2f", j, s) for j in "omp" for s in (1, -1)]
    + [("P2f", "a", 1), ("P2f", "b", -1)]
)
IDS = {key: at for at, key in enumerate(KEYS)}


class Tree:
    def __init__(self, me, way, blocks, send_sem, recv_sem):
        self.y, self.x, self.way = me // SIDE, lax.rem(me, SIDE), way
        self.blocks, self.send_sem, self.recv_sem = blocks, send_sem, recv_sem
        self.memo = {}
        self.slots = {}
        for half in (0, 1):
            for first in range(SIDE):
                for second in range(SIDE):
                    self.slot(half, first, second)

    def node(self, half, first, second):
        key = (half, first % SIDE, second % SIDE)
        if key not in self.memo:
            first, second = first * self.way, second * self.way
            dy, dx = (second, first) if half == 0 else (first, second)
            self.memo[key] = wrap(self.y + dy, SIDE) * SIDE + wrap(self.x + dx, SIDE)
        return self.memo[key]

    def slot(self, half, first, second):
        key = (half, first % SIDE, second % SIDE)
        if key not in self.slots:
            node = self.node(half, first, second)
            self.slots[key] = node if half == 0 else lax.rem(node, SIDE) * SIDE + node // SIDE
        return self.slots[key]

    def describe(self, key):
        kind, sign = key[0], key[-1]
        if kind == "P1":
            return (0, 0), 0, 0, sign
        if kind == "P1f":
            return (-sign, 0), sign, 0, sign
        first, part = BLOCK[key[1]]
        if kind == "P2":
            return (first, 0), part, 1, sign
        return (first, -sign), sign, 1, sign

    def copy(self, half, key, receiver=False):
        (first, second), part, axis, sign = self.describe(key)
        if receiver:
            first, second = (first - sign, second) if axis == 0 else (first, second - sign)
        start, rows = PART[part]
        ref = self.blocks.at[half, self.slot(half, first, second), pl.ds(start, rows)]
        to = self.node(half, sign, 0) if axis == 0 else self.node(half, 0, sign)
        return pltpu.make_async_remote_copy(
            src_ref=ref, dst_ref=ref,
            send_sem=self.send_sem.at[half, IDS[key]], recv_sem=self.recv_sem.at[half, IDS[key]],
            device_id={"seq": to}, device_id_type=MESH,
        )

    def start(self, *key):
        for half in (0, 1):
            self.copy(half, key).start()

    def arrive(self, *key):
        for half in (0, 1):
            self.copy(half, key, True).wait_recv()

    def first(self):
        for s in (1, -1):
            self.start("P1", s)
        for s in (1, -1):
            self.start("P2", "o", s)

    def rest(self, done, late):
        for s in (1, -1):
            self.arrive("P1", s)
            self.start("P1f", s)
        for s in (1, -1):
            self.start("P2", "m", s)
            self.start("P2", "p", s)
        done([(-1, 0), (1, 0)])
        for s in (1, -1):
            self.arrive("P2", "o", s)
            self.start("P2f", "o", s)
        for s in (1, -1):
            self.arrive("P1f", s)
            for t in (1, -1):
                self.start("P2", "a" if s == 1 else "b", t)
        done([(0, -1), (0, 1), (2, 0)])
        for j in ("m", "p"):
            for s in (1, -1):
                self.arrive("P2", j, s)
                self.start("P2f", j, s)
        done([(-1, -1), (-1, 1), (1, -1), (1, 1)])
        for j in ("a", "b"):
            for s in (1, -1):
                self.arrive("P2", j, s)
                if ("P2f", j, s) in IDS:
                    self.start("P2f", j, s)
        late()
        for s in (1, -1):
            self.arrive("P2f", "o", s)
        done([(2, -1), (2, 1), (0, 2)])
        for j in ("m", "p"):
            for s in (1, -1):
                self.arrive("P2f", j, s)
        self.arrive("P2f", "a", 1)
        self.arrive("P2f", "b", -1)
        done([(-1, 2), (1, 2), (2, 2)])

    def finish(self):
        for key in KEYS:
            for half in (0, 1):
                self.copy(half, key).wait_send()


QB = 256


def attend(q, kt, k, va, vat, g, att, dq, dkt, dvt, between):
    dkt[...] = jnp.zeros_like(dkt)
    dvt[...] = jnp.zeros_like(dvt)
    lane = lax.broadcasted_iota(jnp.int32, (QB, LANES), 1)

    def block(at, carry):
        between(at)
        rows = pl.ds(at * QB, QB)
        queries = q[rows]
        scores = dot(queries, kt[...])
        weights = jnp.exp2(scores - jnp.max(scores, axis=1, keepdims=True)).astype(BF)
        raw = dot(weights, va[...])
        inverse = 1.0 / raw[:, HEAD:HEAD + 1]
        out = jnp.where(lane < HEAD, raw * inverse, 0.0)
        att[rows] = out.astype(BF)
        scaled = (g[rows].astype(F32) * inverse).astype(BF)
        delta = jnp.sum(scaled.astype(F32) * out, axis=1, keepdims=True)
        high = delta.astype(BF).astype(F32)
        extended = jnp.where(lane == HEAD, -high, scaled.astype(F32))
        extended = jnp.where(lane == HEAD + 1, high - delta, extended).astype(BF)
        d_scores = weights * dot(extended, vat[...]).astype(BF)
        dq[rows] = (dot(d_scores, k[...]) * SCALE).astype(BF)
        dkt[...] += dot(queries, d_scores, 0, 0)
        dvt[...] += dot(scaled, weights, 0, 0)
        return carry

    lax.fori_loop(0, LIVE // QB, block, 0)


HALF_LANES = 768
SHARD = WIDE // DEPTH
FIRST = SEQ * HALF
MORE = SURE - HALF
PACK_AT = FIRST + SEQ * MORE


def layer_kernel(
    tokens_in, w, d_out, rank, index,
    attn_out, d_tokens_out, d_wqkv,
    rows_buf, blocks, normed_buf, inv_buf, w_rows, w_side, w3, g_send, g_recv, qkv,
    q, k, v, g, kt, vt, att, dq, dkt, dvt,
    d_send, att_send, att_recv, d_recv, part_send, part_recv,
    dwt, pair_send, pair_recv, z_send, z_recv, z_all, z_other,
    t_ssem, t_rsem, g_ssem, g_rsem, w_ssem, w_rsem,
    d_ssem, d_rsem, p_ssem, p_rsem, a_ssem, a_rsem, c_ssem, c_rsem, z_ssem, z_rsem, o_ssem, o_rsem,
    in_sem, out_sem,
):
    me = lax.axis_index("seq")
    batch = lax.axis_index("batch")
    core, z = lax.rem(batch, 2), batch // 2
    y, x = me // SIDE, lax.rem(me, SIDE)
    place = (y, x)

    def peer(axis, step):
        if axis == 0:
            return wrap(y + step, SIDE) * SIDE + x
        return y * SIDE + wrap(x + step, SIDE)

    def above(step):
        return wrap(z + step, DEPTH) * 2 + core

    other = batch + 1 - 2 * core

    fetch = pltpu.make_async_copy(tokens_in.at[0], rows_buf, in_sem)
    fetch.start()
    barrier = pltpu.get_barrier_semaphore()
    for step in range(1, SEQ):
        pl.semaphore_signal(
            barrier, inc=1, device_id={"seq": lax.rem(me + step, SEQ)}, device_id_type=MESH
        )
    for step in range(1, DEPTH):
        pl.semaphore_signal(
            barrier, inc=1, device_id={"batch": above(step)}, device_id_type=MESH
        )
    pl.semaphore_signal(barrier, inc=1, device_id={"batch": other}, device_id_type=MESH)

    def remote(src, dst, sems, at, to, where="seq"):
        return pltpu.make_async_remote_copy(
            src_ref=src, dst_ref=dst, send_sem=sems[0].at[at], recv_sem=sems[1].at[at],
            device_id={where: to}, device_id_type=MESH,
        )

    w_sems = (w_ssem, w_rsem)

    def w_own(axis, sign):
        dst = w_side.at[axis, place[axis], :, pl.ds(0, SURE)]
        return remote(w_rows, dst, w_sems, (axis, (1 - sign) // 2), peer(axis, sign))

    def w_from(axis, sign):
        dst = w_side.at[axis, wrap(place[axis] - sign, SIDE), :, pl.ds(0, SURE)]
        return remote(w_rows, dst, w_sems, (axis, (1 - sign) // 2), peer(axis, -sign))

    def w_onward(axis, sign, receiver=False):
        origin = wrap(place[axis] - (2 * sign if receiver else sign), SIDE)
        ref = w_side.at[axis, origin, :, pl.ds(0 if sign == 1 else SURE // 2, SURE // 2)]
        return remote(ref, ref, w_sems, (axis, 2 + (1 - sign) // 2), peer(axis, sign))

    fetch.wait()
    spread = (lax.broadcasted_iota(jnp.int32, (rows_buf.shape[0], CAP), 0) == index[...]).astype(BF)
    picked = dot(spread, rows_buf[...], 0, 0)
    centred = picked - jnp.mean(picked, axis=1, keepdims=True)
    inv_std = lax.rsqrt(jnp.mean(centred * centred, axis=1, keepdims=True) + EPSILON)
    normed = centred * inv_std
    pl.semaphore_wait(barrier, SEQ - 1 + DEPTH)
    blocks[0, me] = normed[:HALF].astype(BF)
    blocks[1, x * SIDE + y] = normed[HALF:].astype(BF)
    tree = Tree(me, 1 - 2 * core, blocks, t_ssem, t_rsem)
    tree.first()
    normed_buf[...] = normed
    inv_buf[...] = jnp.broadcast_to(inv_std, inv_buf.shape)

    g_send[...] = jnp.zeros_like(g_send)
    for head in range(HEADS):
        g_send[head, :, :HEAD] = d_out[0, :, head * HEAD:(head + 1) * HEAD]
    g_sems = (g_ssem, g_rsem)

    def g_copy(step):
        to = lax.rem(me + step, SEQ)
        return remote(g_send.at[to], g_recv.at[me], g_sems, step, to)

    def g_arrival(step):
        origin = lax.rem(me - step + SEQ, SEQ)
        return remote(g_send.at[origin], g_recv.at[origin], g_sems, step, origin)

    def g_start(step, carry):
        g_copy(step).start()
        return carry

    for part in range(3):
        w_rows[part, :HEAD] = w[part * HEAD:(part + 1) * HEAD]
        w_rows[part, HEAD:] = jnp.zeros((SURE - HEAD, D), BF)
    w_side[:, :, :, SURE:, :] = jnp.zeros((2, SIDE, 3, LANES - SURE, D), BF)
    for axis in (0, 1):
        w_side[axis, place[axis], :, :SURE, :] = w_rows[...]
    w3[...] = w_side[0, y].reshape(WIDE, D).T
    g_recv[me] = g_send[me]

    lane = lax.broadcasted_iota(jnp.int32, (1, WIDE), 1)
    column_scale = jnp.where(lane < LANES, SCALE * LOG2E, 1.0).astype(F32)

    def project(offsets):
        places = [(half, tree.slot(half, *offset)) for half in (0, 1) for offset in offsets]
        rows = jnp.concatenate([blocks[at] for at in places], axis=0)
        out = (dot(rows, w3[...]) * column_scale).astype(BF)
        for at, (half, slot) in enumerate(places):
            qkv[half, slot] = out[at * HALF:(at + 1) * HALF]

    project([(0, 0)])
    tree.rest(project, lambda: lax.fori_loop(1, SEQ, g_start, 0))

    def arrival(ref, sems, axis, step):
        part = ref.at[axis, wrap(place[axis] - step, SIDE)]
        return remote(part, part, sems, (axis, step), peer(axis, step))

    def g_wait(step, carry):
        g_copy(step).wait_send()
        g_arrival(step).wait_recv()
        return carry

    lax.fori_loop(1, SEQ, g_wait, 0)
    for axis in (0, 1):
        for sign in (1, -1):
            w_own(axis, sign).start()
    hot = (lax.broadcasted_iota(jnp.int32, (PACKED, HEADS * TAIL), 0) == rank[...]).astype(BF)
    turned = [column * SIDE + row for row in range(SIDE) for column in range(SIDE)]
    g[:FIRST] = g_recv[:, :HALF, :].reshape(FIRST, LANES)
    for at, owner in enumerate(turned):
        g[FIRST + at * MORE:FIRST + (at + 1) * MORE] = g_recv[owner, HALF:SURE, :]
    g_tail = jnp.concatenate([g_recv[owner, SURE:, :] for owner in turned], axis=0)
    g[PACK_AT:] = dot(hot, g_tail).astype(BF)

    tail = dot(hot, qkv[1, :, MORE:, :].reshape(HEADS * TAIL, WIDE)).astype(BF)
    for part, ref in enumerate((q, k, v)):
        lanes = slice(part * LANES, (part + 1) * LANES)
        ref[:FIRST] = qkv[0, :, :, lanes].reshape(FIRST, LANES)
        ref[FIRST:PACK_AT] = qkv[1, :, :MORE, lanes].reshape(SEQ * MORE, LANES)
        ref[PACK_AT:] = tail[:, lanes]
    lane = lax.broadcasted_iota(jnp.int32, (LIVE, LANES), 1)
    ones = (lane == HEAD) | (lane == HEAD + 1)
    v[...] = jnp.where(ones, 1.0, v[...].astype(F32)).astype(BF)
    kt[...] = k[...].T
    vt[...] = v[...].T

    def between(at):
        @pl.when(at == 5)
        def _():
            for axis in (0, 1):
                for sign in (1, -1):
                    w_from(axis, sign).wait_recv()
                    w_onward(axis, sign).start()

    attend(q, kt, k, v, vt, g, att, dq, dkt, dvt, between)

    dk = (dkt[...].T * LN2).astype(BF)
    dv = dvt[...].T.astype(BF)
    packed = jnp.concatenate([dq[PACK_AT:], dk[PACK_AT:], dv[PACK_AT:], att[PACK_AT:]], axis=1)
    loose = dot(hot, packed, 0, 0).astype(BF).reshape(SIDE, SIDE, TAIL, 4 * LANES)
    for part, value in enumerate((dq, dk, dv)):
        lanes = slice(part * LANES, (part + 1) * LANES)
        d_send[0, :, :, :, lanes] = value[:FIRST].reshape(SIDE, SIDE, HALF, LANES)
        d_send[1, :, :, :MORE, lanes] = value[FIRST:PACK_AT].reshape(SIDE, SIDE, MORE, LANES)
    d_send[1, :, :, MORE:, :] = loose[..., :WIDE]

    d_sems = (d_ssem, d_rsem)

    def d_copy(axis, step):
        to = wrap(place[axis] + step, SIDE)
        return remote(
            d_send.at[axis, to], d_recv.at[axis, place[axis]], d_sems, (axis, step), peer(axis, step)
        )

    for step in (2, 1, 3):
        for axis in (0, 1):
            d_copy(axis, step).start()
    for axis in (0, 1):
        d_recv[axis, place[axis]] = d_send[axis, place[axis]]
    att_send[:, :HALF, :] = att[:FIRST].reshape(SEQ, HALF, LANES)
    for at, owner in enumerate(turned):
        att_send[owner, HALF:SURE, :] = att[FIRST + at * MORE:FIRST + (at + 1) * MORE]
        att_send[owner, SURE:, :] = loose[at // SIDE, at % SIDE, :, WIDE:]
    a_sems = (a_ssem, a_rsem)

    def a_copy(step):
        to = lax.rem(me + step, SEQ)
        return remote(att_send.at[to], att_recv.at[me], a_sems, step, to)

    def a_arrival(step):
        origin = lax.rem(me - step + SEQ, SEQ)
        return remote(att_send.at[origin], att_recv.at[origin], a_sems, step, origin)

    def a_start(step, carry):
        a_copy(step).start()
        return carry

    lax.fori_loop(1, SEQ, a_start, 0)
    att_recv[me] = att_send[me]

    for first, last in ((0, 512), (512, 1024), (1024, D)):
        dwt[:, first:last] = dot(
            d_send[...].reshape(SEQ * CAP, WIDE),
            blocks[:, :, :, first:last].reshape(SEQ * CAP, last - first), 0, 0,
        )

    def lanes_of(which):
        return pl.ds(pl.multiple_of(which * (D - HALF_LANES), LANES), HALF_LANES)

    pair_send[...] = dwt[:, lanes_of(1 - core)].astype(BF)
    c_sems = (c_ssem, c_rsem)
    pair_copy = remote(pair_send, pair_recv, c_sems, 0, other, "batch")
    pair_copy.start()

    z_sems = (z_ssem, z_rsem)

    def z_copy(phase, step):
        src = z_send.at[wrap(z + step, DEPTH)] if phase == 0 else z_all.at[z]
        dst = (z_recv if phase == 0 else z_all).at[z]
        return remote(src, dst, z_sems, (phase, step), above(step), "batch")

    def z_arrival(phase, step):
        ref = (z_recv if phase == 0 else z_all).at[wrap(z - step, DEPTH)]
        return remote(ref, ref, z_sems, (phase, step), above(step), "batch")

    p_sems = (p_ssem, p_rsem)

    def p_copy(axis, step):
        to = wrap(place[axis] + step, SIDE)
        return remote(
            part_send.at[axis, to], part_recv.at[axis, place[axis]], p_sems, (axis, step), peer(axis, step)
        )

    for axis in (0, 1):
        for sign in (1, -1):
            w_onward(axis, sign, True).wait_recv()
        for step in (1, 2, 3):
            arrival(d_recv, d_sems, axis, step).wait_recv()
        left = jnp.concatenate(
            [d_recv[axis, head].reshape(SIDE * HALF, WIDE) for head in range(SIDE)], axis=1
        )
        partial = dot(left, w_side[axis].reshape(SIDE * WIDE, D))
        part_send[1 - axis] = partial.astype(BF).reshape(SIDE, HALF, D)
        for step in (2, 1, 3):
            p_copy(1 - axis, step).start()
        if axis == 0:
            pair_copy.wait()
            z_send[...] = (dwt[:, lanes_of(core)] + pair_recv[...].astype(F32)).astype(BF).reshape(
                DEPTH, SHARD, HALF_LANES
            )
            for step in (4, 3, 5, 2, 6, 1, 7):
                z_copy(0, step).start()
            z_recv[z] = z_send[z]
    for axis in (0, 1):
        part_recv[axis, place[axis]] = part_send[axis, place[axis]]

    def a_wait(step, carry):
        a_copy(step).wait_send()
        a_arrival(step).wait_recv()
        return carry

    lax.fori_loop(1, SEQ, a_wait, 0)
    for head in range(HEADS):
        attn_out[0, :, head * HEAD:(head + 1) * HEAD] = att_recv[head, :, :HEAD]

    for step in range(1, DEPTH):
        z_arrival(0, step).wait_recv()
    total = z_recv[0].astype(F32)
    for at in range(1, DEPTH):
        total = total + z_recv[at].astype(F32)
    z_all[z] = total.astype(BF)
    for step in (4, 3, 5, 2, 6, 1, 7):
        z_copy(1, step).start()

    def o_copy(step):
        slot = wrap(z - step, DEPTH)
        return remote(z_all.at[slot], z_other.at[slot], (o_ssem, o_rsem), step, other, "batch")

    o_copy(0).start()

    for axis in (0, 1):
        for step in (1, 2, 3):
            arrival(part_recv, p_sems, axis, step).wait_recv()
    halves = []
    for axis in (1, 0):
        value = part_recv[axis, 0].astype(F32)
        for at in range(1, SIDE):
            value = value + part_recv[axis, at].astype(F32)
        halves.append(value)
    d_normed = jnp.concatenate(halves, axis=0)
    normed = normed_buf[...]
    d_picked = inv_buf[:, :1] * (
        d_normed
        - jnp.mean(d_normed, axis=1, keepdims=True)
        - normed * jnp.mean(d_normed * normed, axis=1, keepdims=True)
    )
    spread = (lax.broadcasted_iota(jnp.int32, (rows_buf.shape[0], CAP), 0) == index[...]).astype(BF)
    rows_buf[...] = dot(spread, d_picked.astype(BF)).astype(BF)
    store = pltpu.make_async_copy(rows_buf, d_tokens_out.at[0], out_sem)
    store.start()

    for step in (1, 7, 2, 6, 3, 5, 4):
        z_arrival(1, step).wait_recv()
        o_copy(step).start()
    for step in range(DEPTH):
        o_copy(step).wait()
    mine, theirs = (
        ref[...].astype(F32).reshape(WIDE, HALF_LANES) for ref in (z_all, z_other)
    )
    low = jnp.where(core == 0, mine, theirs)
    high = jnp.where(core == 0, theirs, mine)
    overlap = 2 * HALF_LANES - D
    for part in range(3):
        rows = slice(part * HEAD, (part + 1) * HEAD)
        padded = slice(part * LANES, part * LANES + HEAD)
        d_wqkv[rows, :HALF_LANES] = low[padded]
        d_wqkv[rows, HALF_LANES:] = high[padded, overlap:]

    for axis in (0, 1):
        for sign in (1, -1):
            w_own(axis, sign).wait_send()
            w_onward(axis, sign).wait_send()
        for step in (1, 2, 3):
            d_copy(axis, step).wait_send()
            p_copy(axis, step).wait_send()
    for step in range(1, DEPTH):
        z_copy(0, step).wait_send()
        z_copy(1, step).wait_send()
    tree.finish()
    store.wait()


def layer_call(tokens, w, d_out, rank, index):
    vmem = pl.BlockSpec(memory_space=VMEM)
    anywhere = pl.BlockSpec(memory_space=pl.ANY)
    dma = pltpu.SemaphoreType.DMA
    positions = tokens.shape[1]
    pair = [dma((2, SIDE)), dma((2, SIDE))]
    return pl.pallas_call(
        layer_kernel,
        out_shape=(
            jax.ShapeDtypeStruct((1, CAP, D), BF),
            jax.ShapeDtypeStruct((1, positions, D), BF),
            jax.ShapeDtypeStruct((3 * HEAD, D), F32),
        ),
        in_specs=[anywhere] + [vmem] * 4,
        out_specs=(vmem, anywhere, vmem),
        scratch_shapes=[
            VMEM((positions, D), BF),
            VMEM((2, SEQ, HALF, D), BF),
            VMEM((CAP, D), F32),
            VMEM((CAP, LANES), F32),
            VMEM((3, SURE, D), BF),
            VMEM((2, SIDE, 3, LANES, D), BF),
            VMEM((D, WIDE), BF),
            VMEM((SEQ, CAP, LANES), BF),
            VMEM((SEQ, CAP, LANES), BF),
            VMEM((2, SEQ, HALF, WIDE), BF),
            VMEM((LIVE, LANES), BF),
            VMEM((LIVE, LANES), BF),
            VMEM((LIVE, LANES), BF),
            VMEM((LIVE, LANES), BF),
            VMEM((LANES, LIVE), BF),
            VMEM((LANES, LIVE), BF),
            VMEM((LIVE, LANES), BF),
            VMEM((LIVE, LANES), BF),
            VMEM((LANES, LIVE), F32),
            VMEM((LANES, LIVE), F32),
            VMEM((2, SIDE, SIDE, HALF, WIDE), BF),
            VMEM((SEQ, CAP, LANES), BF),
            VMEM((SEQ, CAP, LANES), BF),
            VMEM((2, SIDE, SIDE, HALF, WIDE), BF),
            VMEM((2, SIDE, HALF, D), BF),
            VMEM((2, SIDE, HALF, D), BF),
            VMEM((WIDE, D), F32),
            VMEM((WIDE, HALF_LANES), BF),
            VMEM((WIDE, HALF_LANES), BF),
            VMEM((DEPTH, SHARD, HALF_LANES), BF),
            VMEM((DEPTH, SHARD, HALF_LANES), BF),
            VMEM((DEPTH, SHARD, HALF_LANES), BF),
            VMEM((DEPTH, SHARD, HALF_LANES), BF),
            dma((2, len(KEYS))), dma((2, len(KEYS))),
            dma((SEQ,)), dma((SEQ,)),
            *pair, *pair, *pair,
            dma((SEQ,)), dma((SEQ,)),
            dma((2,)), dma((2,)),
            dma((2, DEPTH)), dma((2, DEPTH)),
            dma((DEPTH,)), dma((DEPTH,)),
            dma, dma,
        ],
        compiler_params=pltpu.CompilerParams(
            collective_id=1, has_side_effects=True, vmem_limit_bytes=VMEM_BYTES
        ),
        name="layer",
    )(tokens, w, d_out, rank, index)


def per_device(tokens, w_qkv, vis_index, counts, d_out):
    extra = (counts[0] - SURE).reshape(SIDE, SIDE).T.reshape(SEQ)
    order = jnp.arange(SEQ, dtype=jnp.int32)
    before = jnp.sum(jnp.where(order[None, :] < order[:, None], extra[None, :], 0), axis=1)
    within = jnp.arange(TAIL, dtype=jnp.int32)
    rank = jnp.where(within[None, :] < extra[:, None], before[:, None] + within[None, :], -1)
    rank = rank.reshape(1, SEQ * TAIL).astype(jnp.int32)
    attn_out, d_tokens, d_wqkv = layer_call(tokens, w_qkv.T, d_out, rank, vis_index)
    return attn_out, d_tokens, d_wqkv.T


def solution(mesh):
    placed = (
        P("batch", "seq", None),
        P(None, "seq"),
        P("batch", "seq"),
        P("batch", None),
        P("batch", "seq", None),
    )
    return jax.shard_map(
        per_device,
        mesh=mesh,
        in_specs=placed,
        out_specs=(P("batch", "seq", None), P("batch", "seq", None), P(None, "seq")),
        check_vma=False,
    )
```

```python
import jax
import jax.numpy as jnp
from jax import lax
from jax.experimental import pallas as pl
from jax.experimental.pallas import tpu as pltpu
from jax.sharding import PartitionSpec as P

D = 1408
HEAD = 88
HEADS = 16
CAP = 160
HALF = 80
SURE = 96
TAIL = CAP - SURE
LIVE = 2048
PACKED = LIVE - HEADS * SURE
LANES = 128
WIDE = 3 * LANES
SEQ = 16
SIDE = 4
DEPTH = 8
EPSILON = 1e-06
LOG2E = 1.4426950408889634
LN2 = 0.6931471805599453
SCALE = HEAD ** (-0.5)
MESH = pl.DeviceIdType.MESH
BF = jnp.bfloat16
F32 = jnp.float32
VMEM = pltpu.VMEM
VMEM_BYTES = 62 * 2**20
CHUNKS = 4
CHUNK = 1024 // CHUNKS


def dot(left, right, left_dim=1, right_dim=0):
    return lax.dot_general(
        left, right, (((left_dim,), (right_dim,)), ((), ())), preferred_element_type=F32
    )


def wrap(value, size):
    return lax.rem(value + 2 * size, size)


PART = {0: (0, 80), 1: (0, 48), -1: (48, 32)}
BLOCK = {"o": (0, 0), "m": (-1, 0), "p": (1, 0), "a": (2, 1), "b": (2, -1)}
KEYS = (
    [("P1", s) for s in (1, -1)]
    + [("P1f", s) for s in (1, -1)]
    + [("P2", j, s) for j in "ompab" for s in (1, -1)]
    + [("P2f", j, s) for j in "omp" for s in (1, -1)]
    + [("P2f", "a", 1), ("P2f", "b", -1)]
)
IDS = {key: at for at, key in enumerate(KEYS)}


class Tree:
    def __init__(self, me, way, blocks, send_sem, recv_sem):
        self.y, self.x, self.way = me // SIDE, lax.rem(me, SIDE), way
        self.blocks, self.send_sem, self.recv_sem = blocks, send_sem, recv_sem
        self.memo = {}
        self.slots = {}
        for half in (0, 1):
            for first in range(SIDE):
                for second in range(SIDE):
                    self.slot(half, first, second)

    def node(self, half, first, second):
        key = (half, first % SIDE, second % SIDE)
        if key not in self.memo:
            first, second = first * self.way, second * self.way
            dy, dx = (second, first) if half == 0 else (first, second)
            self.memo[key] = wrap(self.y + dy, SIDE) * SIDE + wrap(self.x + dx, SIDE)
        return self.memo[key]

    def slot(self, half, first, second):
        key = (half, first % SIDE, second % SIDE)
        if key not in self.slots:
            node = self.node(half, first, second)
            self.slots[key] = node if half == 0 else lax.rem(node, SIDE) * SIDE + node // SIDE
        return self.slots[key]

    def describe(self, key):
        kind, sign = key[0], key[-1]
        if kind == "P1":
            return (0, 0), 0, 0, sign
        if kind == "P1f":
            return (-sign, 0), sign, 0, sign
        first, part = BLOCK[key[1]]
        if kind == "P2":
            return (first, 0), part, 1, sign
        return (first, -sign), sign, 1, sign

    def copy(self, half, key, receiver=False):
        (first, second), part, axis, sign = self.describe(key)
        if receiver:
            first, second = (first - sign, second) if axis == 0 else (first, second - sign)
        start, rows = PART[part]
        ref = self.blocks.at[half, self.slot(half, first, second), pl.ds(start, rows)]
        to = self.node(half, sign, 0) if axis == 0 else self.node(half, 0, sign)
        return pltpu.make_async_remote_copy(
            src_ref=ref, dst_ref=ref,
            send_sem=self.send_sem.at[half, IDS[key]], recv_sem=self.recv_sem.at[half, IDS[key]],
            device_id={"seq": to}, device_id_type=MESH,
        )

    def start(self, *key):
        for half in (0, 1):
            self.copy(half, key).start()

    def arrive(self, *key):
        for half in (0, 1):
            self.copy(half, key, True).wait_recv()

    def first(self):
        for s in (1, -1):
            self.start("P1", s)
        for s in (1, -1):
            self.start("P2", "o", s)

    def rest(self, done):
        for s in (1, -1):
            self.arrive("P1", s)
            self.start("P1f", s)
        for s in (1, -1):
            self.start("P2", "m", s)
            self.start("P2", "p", s)
        done([(-1, 0), (1, 0)])
        for s in (1, -1):
            self.arrive("P2", "o", s)
            self.start("P2f", "o", s)
        for s in (1, -1):
            self.arrive("P1f", s)
            for t in (1, -1):
                self.start("P2", "a" if s == 1 else "b", t)
        done([(0, -1), (0, 1), (2, 0)])
        for j in ("m", "p"):
            for s in (1, -1):
                self.arrive("P2", j, s)
                self.start("P2f", j, s)
        done([(-1, -1), (-1, 1), (1, -1), (1, 1)])
        for j in ("a", "b"):
            for s in (1, -1):
                self.arrive("P2", j, s)
                if ("P2f", j, s) in IDS:
                    self.start("P2f", j, s)
        for s in (1, -1):
            self.arrive("P2f", "o", s)
        done([(2, -1), (2, 1), (0, 2)])
        for j in ("m", "p"):
            for s in (1, -1):
                self.arrive("P2f", j, s)
        self.arrive("P2f", "a", 1)
        self.arrive("P2f", "b", -1)
        done([(-1, 2), (1, 2), (2, 2)])

    def finish(self):
        for key in KEYS:
            for half in (0, 1):
                self.copy(half, key).wait_send()


QB = 256


def attend(q, kt, k, va, vat, g, att, dq, dkt, dvt, between):
    dkt[...] = jnp.zeros_like(dkt)
    dvt[...] = jnp.zeros_like(dvt)
    lane = lax.broadcasted_iota(jnp.int32, (QB, LANES), 1)

    def block(at, carry):
        between(at)
        rows = pl.ds(at * QB, QB)
        queries = q[rows]
        scores = dot(queries, kt[...])
        weights = jnp.exp2(scores - jnp.max(scores, axis=1, keepdims=True)).astype(BF)
        raw = dot(weights, va[...])
        inverse = 1.0 / raw[:, HEAD:HEAD + 1]
        out = jnp.where(lane < HEAD, raw * inverse, 0.0)
        att[rows] = out.astype(BF)
        scaled = (g[rows].astype(F32) * inverse).astype(BF)
        delta = jnp.sum(scaled.astype(F32) * out, axis=1, keepdims=True)
        high = delta.astype(BF).astype(F32)
        extended = jnp.where(lane == HEAD, -high, scaled.astype(F32))
        extended = jnp.where(lane == HEAD + 1, high - delta, extended).astype(BF)
        d_scores = weights * dot(extended, vat[...]).astype(BF)
        dq[rows] = (dot(d_scores, k[...]) * SCALE).astype(BF)
        dkt[...] += dot(queries, d_scores, 0, 0)
        dvt[...] += dot(scaled, weights, 0, 0)
        return carry

    lax.fori_loop(0, LIVE // QB, block, 0)


HALF_LANES = 768
SHARD = WIDE // DEPTH
FIRST = SEQ * HALF
MORE = SURE - HALF
PACK_AT = FIRST + SEQ * MORE


def layer_kernel(
    tokens_in, w, d_out, rank, index,
    attn_out, d_tokens_out, d_wqkv,
    rows_buf, blocks, normed_buf, inv_buf, w_side, w3, g_send, g_recv, qkv,
    q, k, v, g, kt, vt, att, dq, dkt, dvt,
    d_send, att_send, att_recv, d_recv, part_send, part_recv,
    turned_d, own_sum, pair_send, pair_recv, z_send, z_recv, z_all, z_other,
    t_ssem, t_rsem, g_ssem, g_rsem, w_ssem, w_rsem,
    d_ssem, d_rsem, p_ssem, p_rsem, a_ssem, a_rsem, c_ssem, c_rsem, z_ssem, z_rsem, o_ssem, o_rsem,
    in_sem, out_sem,
):
    me = lax.axis_index("seq")
    batch = lax.axis_index("batch")
    core, z = lax.rem(batch, 2), batch // 2
    y, x = me // SIDE, lax.rem(me, SIDE)
    place = (y, x)

    def peer(axis, step):
        if axis == 0:
            return wrap(y + step, SIDE) * SIDE + x
        return y * SIDE + wrap(x + step, SIDE)

    def above(step):
        return wrap(z + step, DEPTH) * 2 + core

    other = batch + 1 - 2 * core

    def fetch(part):
        rows = pl.ds(part * CHUNK, CHUNK)
        return pltpu.make_async_copy(tokens_in.at[0, rows], rows_buf.at[rows], in_sem.at[part])

    for part in range(CHUNKS):
        fetch(part).start()
    barrier = pltpu.get_barrier_semaphore()
    for step in range(1, SEQ):
        pl.semaphore_signal(
            barrier, inc=1, device_id={"seq": lax.rem(me + step, SEQ)}, device_id_type=MESH
        )
    for step in range(1, DEPTH):
        pl.semaphore_signal(
            barrier, inc=1, device_id={"batch": above(step)}, device_id_type=MESH
        )
    pl.semaphore_signal(barrier, inc=1, device_id={"batch": other}, device_id_type=MESH)

    def remote(src, dst, sems, at, to, where="seq"):
        return pltpu.make_async_remote_copy(
            src_ref=src, dst_ref=dst, send_sem=sems[0].at[at], recv_sem=sems[1].at[at],
            device_id={where: to}, device_id_type=MESH,
        )

    g_send[...] = jnp.zeros_like(g_send)
    for head in range(HEADS):
        g_send[head, :, :HEAD] = d_out[0, :, head * HEAD:(head + 1) * HEAD]
    g_sems = (g_ssem, g_rsem)

    def g_copy(step):
        to = lax.rem(me + step, SEQ)
        return remote(g_send.at[to], g_recv.at[me], g_sems, step, to)

    def g_arrival(step):
        origin = lax.rem(me - step + SEQ, SEQ)
        return remote(g_send.at[origin], g_recv.at[origin], g_sems, step, origin)

    def g_start(step, carry):
        g_copy(step).start()
        return carry

    pl.semaphore_wait(barrier, SEQ - 1 + DEPTH)
    lax.fori_loop(1, SEQ, g_start, 0)

    column = jnp.broadcast_to(index[...], (LANES, CAP)).T
    lane = lax.broadcasted_iota(jnp.int32, (CAP, LANES), 1)
    picked = None
    for part in range(CHUNKS):
        hot = jnp.concatenate(
            [
                (column == lane + (part * CHUNK + first)).astype(BF)
                for first in range(0, CHUNK, LANES)
            ],
            axis=1,
        )
        fetch(part).wait()
        rows = dot(hot, rows_buf[part * CHUNK:(part + 1) * CHUNK])
        picked = rows if picked is None else picked + rows
    centred = picked - jnp.mean(picked, axis=1, keepdims=True)
    inv_std = lax.rsqrt(jnp.mean(centred * centred, axis=1, keepdims=True) + EPSILON)
    normed = centred * inv_std
    blocks[0, me] = normed[:HALF].astype(BF)
    blocks[1, x * SIDE + y] = normed[HALF:].astype(BF)
    tree = Tree(me, 1 - 2 * core, blocks, t_ssem, t_rsem)
    tree.first()
    normed_buf[...] = normed
    inv_buf[...] = jnp.broadcast_to(inv_std, inv_buf.shape)

    w_side[:, :, :, SURE:, :] = jnp.zeros((2, SIDE, 3, LANES - SURE, D), BF)
    for axis in (0, 1):
        for part in range(3):
            w_side[axis, place[axis], part, :HEAD] = w[part * HEAD:(part + 1) * HEAD]
            w_side[axis, place[axis], part, HEAD:SURE] = jnp.zeros((SURE - HEAD, D), BF)
    w3[...] = w_side[0, y].reshape(WIDE, D).T
    g_recv[me] = g_send[me]

    lane = lax.broadcasted_iota(jnp.int32, (1, WIDE), 1)
    column_scale = jnp.where(lane < LANES, SCALE * LOG2E, 1.0).astype(F32)

    def project(offsets):
        places = [(half, tree.slot(half, *offset)) for half in (0, 1) for offset in offsets]
        rows = jnp.concatenate([blocks[at] for at in places], axis=0)
        out = (dot(rows, w3[...]) * column_scale).astype(BF)
        for at, (half, slot) in enumerate(places):
            qkv[half, slot] = out[at * HALF:(at + 1) * HALF]

    project([(0, 0)])
    tree.rest(project)

    w_sems = (w_ssem, w_rsem)
    way = 1 - 2 * core
    share = SURE // 2
    PIECE = {0: (0, share), 1: (0, 32), -1: (32, share - 32)}

    def w_part(axis, step, piece, whose):
        start, rows = PIECE[piece]
        start = pl.multiple_of(whose * share + start, 16)
        return w_side.at[axis, wrap(place[axis] + step, SIDE), :, pl.ds(start, rows)]

    def w_move(ref, axis, slot, sign, to, where="seq"):
        return remote(ref, ref, w_sems, (axis, slot + (1 - sign) // 2), to, where)

    def w_own(axis, sign):
        return w_move(w_part(axis, 0, 0, core), axis, 0, sign, peer(axis, sign * way))

    def w_from(axis, sign):
        return w_move(w_part(axis, -sign * way, 0, core), axis, 0, sign, peer(axis, -sign * way))

    def w_onward(axis, sign, hops=1):
        return w_move(w_part(axis, -hops * sign * way, sign, core), axis, 2, sign, peer(axis, sign * way))

    def w_across(axis, sign, far, receiver=False):
        whose, side = (1 - core, -way) if receiver else (core, way)
        step, piece = (-2 * sign * side, sign) if far else (-sign * side, 0)
        return w_move(w_part(axis, step, piece, whose), axis, 6 if far else 4, sign, other, "batch")

    def arrival(ref, sems, axis, step):
        part = ref.at[axis, wrap(place[axis] - step, SIDE)]
        return remote(part, part, sems, (axis, step), peer(axis, step))

    def g_wait(step, carry):
        g_copy(step).wait_send()
        g_arrival(step).wait_recv()
        return carry

    lax.fori_loop(1, SEQ, g_wait, 0)
    for axis in (0, 1):
        for sign in (1, -1):
            w_own(axis, sign).start()
    hot = (lax.broadcasted_iota(jnp.int32, (PACKED, HEADS * TAIL), 0) == rank[...]).astype(BF)
    turned = [column * SIDE + row for row in range(SIDE) for column in range(SIDE)]
    g[:FIRST] = g_recv[:, :HALF, :].reshape(FIRST, LANES)
    for at, owner in enumerate(turned):
        g[FIRST + at * MORE:FIRST + (at + 1) * MORE] = g_recv[owner, HALF:SURE, :]
    g_tail = jnp.concatenate([g_recv[owner, SURE:, :] for owner in turned], axis=0)
    g[PACK_AT:] = dot(hot, g_tail).astype(BF)

    tail = dot(hot, qkv[1, :, MORE:, :].reshape(HEADS * TAIL, WIDE)).astype(BF)
    for part, ref in enumerate((q, k, v)):
        lanes = slice(part * LANES, (part + 1) * LANES)
        ref[:FIRST] = qkv[0, :, :, lanes].reshape(FIRST, LANES)
        ref[FIRST:PACK_AT] = qkv[1, :, :MORE, lanes].reshape(SEQ * MORE, LANES)
        ref[PACK_AT:] = tail[:, lanes]
    lane = lax.broadcasted_iota(jnp.int32, (LIVE, LANES), 1)
    ones = (lane == HEAD) | (lane == HEAD + 1)
    v[...] = jnp.where(ones, 1.0, v[...].astype(F32)).astype(BF)
    kt[...] = k[...].T
    vt[...] = v[...].T

    a_sems = (a_ssem, a_rsem)

    def a_part(ref, half, node):
        return ref.at[node, pl.ds(half * HALF, HALF)]

    def a_copy(half, step):
        to = lax.rem(me + step, SEQ)
        return remote(a_part(att_send, half, to), a_part(att_recv, half, me), a_sems, (half, step), to)

    def a_arrival(half, step):
        origin = lax.rem(me - step + SEQ, SEQ)
        part = a_part(att_recv, half, origin)
        return remote(part, part, a_sems, (half, step), origin)

    def a_start(half):
        def one(step, carry):
            a_copy(half, step).start()
            return carry

        lax.fori_loop(1, SEQ, one, 0)

    def between(at):
        @pl.when(at == 4)
        def _():
            for axis in (0, 1):
                for sign in (1, -1):
                    w_from(axis, sign).wait_recv()
                    w_onward(axis, sign).start()
            for axis in (0, 1):
                for sign in (1, -1):
                    w_across(axis, sign, False).start()

        @pl.when(at == FIRST // QB)
        def _():
            att_send[:, :HALF, :] = att[:FIRST].reshape(SEQ, HALF, LANES)
            a_start(0)

        @pl.when(at == LIVE // QB - 1)
        def _():
            for axis in (0, 1):
                for sign in (1, -1):
                    w_onward(axis, sign, 2).wait_recv()
                    w_across(axis, sign, True).start()

    attend(q, kt, k, v, vt, g, att, dq, dkt, dvt, between)

    dk = (dkt[...].T * LN2).astype(BF)
    dv = dvt[...].T.astype(BF)
    packed = jnp.concatenate([dq[PACK_AT:], dk[PACK_AT:], dv[PACK_AT:], att[PACK_AT:]], axis=1)
    loose = dot(hot, packed, 0, 0).astype(BF).reshape(SIDE, SIDE, TAIL, 4 * LANES)
    for part, value in enumerate((dq, dk, dv)):
        lanes = slice(part * LANES, (part + 1) * LANES)
        d_send[0, :, :, :, lanes] = value[:FIRST].reshape(SIDE, SIDE, HALF, LANES)
        d_send[1, :, :, :MORE, lanes] = value[FIRST:PACK_AT].reshape(SIDE, SIDE, MORE, LANES)
    d_send[1, :, :, MORE:, :] = loose[..., :WIDE]

    d_sems = (d_ssem, d_rsem)

    def d_copy(axis, step):
        to = wrap(place[axis] + step, SIDE)
        return remote(
            d_send.at[axis, to], d_recv.at[axis, place[axis]], d_sems, (axis, step), peer(axis, step)
        )

    for step in (2, 1, 3):
        for axis in (0, 1):
            d_copy(axis, step).start()
    for axis in (0, 1):
        d_recv[axis, place[axis]] = d_send[axis, place[axis]]

    def lanes_of(which):
        return pl.ds(pl.multiple_of(which * (D - HALF_LANES), LANES), HALF_LANES)

    turned_d[...] = d_send[...].reshape(SEQ * CAP, WIDE).T

    def product(which):
        return dot(turned_d[...], blocks[:, :, :, lanes_of(which)].reshape(SEQ * CAP, HALF_LANES))

    pair_send[...] = product(1 - core).astype(BF)
    c_sems = (c_ssem, c_rsem)
    pair_copy = remote(pair_send, pair_recv, c_sems, 0, other, "batch")
    pair_copy.start()
    for at, owner in enumerate(turned):
        att_send[owner, HALF:SURE, :] = att[FIRST + at * MORE:FIRST + (at + 1) * MORE]
        att_send[owner, SURE:, :] = loose[at // SIDE, at % SIDE, :, WIDE:]
    a_start(1)
    att_recv[me] = att_send[me]
    own_sum[...] = product(core)

    z_sems = (z_ssem, z_rsem)

    def z_copy(phase, step):
        src = z_send.at[wrap(z + step, DEPTH)] if phase == 0 else z_all.at[z]
        dst = (z_recv if phase == 0 else z_all).at[z]
        return remote(src, dst, z_sems, (phase, step), above(step), "batch")

    def z_arrival(phase, step):
        ref = (z_recv if phase == 0 else z_all).at[wrap(z - step, DEPTH)]
        return remote(ref, ref, z_sems, (phase, step), above(step), "batch")

    pair_copy.wait()
    z_send[...] = (own_sum[...] + pair_recv[...].astype(F32)).astype(BF).reshape(
        DEPTH, SHARD, HALF_LANES
    )
    for step in (4, 3, 5, 2, 6, 1, 7):
        z_copy(0, step).start()
    z_recv[z] = z_send[z]

    p_sems = (p_ssem, p_rsem)

    def p_copy(axis, step):
        to = wrap(place[axis] + step, SIDE)
        return remote(
            part_send.at[axis, to], part_recv.at[axis, place[axis]], p_sems, (axis, step), peer(axis, step)
        )

    for axis in (0, 1):
        for sign in (1, -1):
            w_across(axis, sign, False, True).wait_recv()
            w_across(axis, sign, True, True).wait_recv()
        for step in (1, 2, 3):
            arrival(d_recv, d_sems, axis, step).wait_recv()
        left = jnp.concatenate(
            [d_recv[axis, head].reshape(SIDE * HALF, WIDE) for head in range(SIDE)], axis=1
        )
        partial = dot(left, w_side[axis].reshape(SIDE * WIDE, D))
        part_send[1 - axis] = partial.astype(BF).reshape(SIDE, HALF, D)
        for step in (2, 1, 3):
            p_copy(1 - axis, step).start()
    for axis in (0, 1):
        part_recv[axis, place[axis]] = part_send[axis, place[axis]]

    def a_wait(step, carry):
        for half in (0, 1):
            a_copy(half, step).wait_send()
            a_arrival(half, step).wait_recv()
        return carry

    lax.fori_loop(1, SEQ, a_wait, 0)
    for head in range(HEADS):
        attn_out[0, :, head * HEAD:(head + 1) * HEAD] = att_recv[head, :, :HEAD]

    for step in range(1, DEPTH):
        z_arrival(0, step).wait_recv()
    total = z_recv[0].astype(F32)
    for at in range(1, DEPTH):
        total = total + z_recv[at].astype(F32)
    z_all[z] = total.astype(BF)
    for step in (4, 3, 5, 2, 6, 1, 7):
        z_copy(1, step).start()

    def o_copy(step):
        slot = wrap(z - step, DEPTH)
        return remote(z_all.at[slot], z_other.at[slot], (o_ssem, o_rsem), step, other, "batch")

    o_copy(0).start()

    for axis in (0, 1):
        for step in (1, 2, 3):
            arrival(part_recv, p_sems, axis, step).wait_recv()
    halves = []
    for axis in (1, 0):
        value = part_recv[axis, 0].astype(F32)
        for at in range(1, SIDE):
            value = value + part_recv[axis, at].astype(F32)
        halves.append(value)
    d_normed = jnp.concatenate(halves, axis=0)
    normed = normed_buf[...]
    d_picked = inv_buf[:, :1] * (
        d_normed
        - jnp.mean(d_normed, axis=1, keepdims=True)
        - normed * jnp.mean(d_normed * normed, axis=1, keepdims=True)
    )
    spread = (lax.broadcasted_iota(jnp.int32, (rows_buf.shape[0], CAP), 0) == index[...]).astype(BF)
    rows_buf[...] = dot(spread, d_picked.astype(BF)).astype(BF)
    store = pltpu.make_async_copy(rows_buf, d_tokens_out.at[0], out_sem)
    store.start()

    for step in (1, 7, 2, 6, 3, 5, 4):
        z_arrival(1, step).wait_recv()
        o_copy(step).start()
    for step in range(DEPTH):
        o_copy(step).wait()
    mine, theirs = (
        ref[...].astype(F32).reshape(WIDE, HALF_LANES) for ref in (z_all, z_other)
    )
    low = jnp.where(core == 0, mine, theirs)
    high = jnp.where(core == 0, theirs, mine)
    overlap = 2 * HALF_LANES - D
    for part in range(3):
        rows = slice(part * HEAD, (part + 1) * HEAD)
        padded = slice(part * LANES, part * LANES + HEAD)
        d_wqkv[rows, :HALF_LANES] = low[padded]
        d_wqkv[rows, HALF_LANES:] = high[padded, overlap:]

    for axis in (0, 1):
        for sign in (1, -1):
            w_own(axis, sign).wait_send()
            w_onward(axis, sign).wait_send()
            w_across(axis, sign, False).wait_send()
            w_across(axis, sign, True).wait_send()
        for step in (1, 2, 3):
            d_copy(axis, step).wait_send()
            p_copy(axis, step).wait_send()
    for step in range(1, DEPTH):
        z_copy(0, step).wait_send()
        z_copy(1, step).wait_send()
    tree.finish()
    store.wait()


def layer_call(tokens, w, d_out, rank, index):
    vmem = pl.BlockSpec(memory_space=VMEM)
    anywhere = pl.BlockSpec(memory_space=pl.ANY)
    dma = pltpu.SemaphoreType.DMA
    positions = tokens.shape[1]
    pair = [dma((2, SIDE)), dma((2, SIDE))]
    return pl.pallas_call(
        layer_kernel,
        out_shape=(
            jax.ShapeDtypeStruct((1, CAP, D), BF),
            jax.ShapeDtypeStruct((1, positions, D), BF),
            jax.ShapeDtypeStruct((3 * HEAD, D), F32),
        ),
        in_specs=[anywhere] + [vmem] * 4,
        out_specs=(vmem, anywhere, vmem),
        scratch_shapes=[
            VMEM((positions, D), BF),
            VMEM((2, SEQ, HALF, D), BF),
            VMEM((CAP, D), F32),
            VMEM((CAP, LANES), F32),
            VMEM((2, SIDE, 3, LANES, D), BF),
            VMEM((D, WIDE), BF),
            VMEM((SEQ, CAP, LANES), BF),
            VMEM((SEQ, CAP, LANES), BF),
            VMEM((2, SEQ, HALF, WIDE), BF),
            VMEM((LIVE, LANES), BF),
            VMEM((LIVE, LANES), BF),
            VMEM((LIVE, LANES), BF),
            VMEM((LIVE, LANES), BF),
            VMEM((LANES, LIVE), BF),
            VMEM((LANES, LIVE), BF),
            VMEM((LIVE, LANES), BF),
            VMEM((LIVE, LANES), BF),
            VMEM((LANES, LIVE), F32),
            VMEM((LANES, LIVE), F32),
            VMEM((2, SIDE, SIDE, HALF, WIDE), BF),
            VMEM((SEQ, CAP, LANES), BF),
            VMEM((SEQ, CAP, LANES), BF),
            VMEM((2, SIDE, SIDE, HALF, WIDE), BF),
            VMEM((2, SIDE, HALF, D), BF),
            VMEM((2, SIDE, HALF, D), BF),
            VMEM((WIDE, SEQ * CAP), BF),
            VMEM((WIDE, HALF_LANES), F32),
            VMEM((WIDE, HALF_LANES), BF),
            VMEM((WIDE, HALF_LANES), BF),
            VMEM((DEPTH, SHARD, HALF_LANES), BF),
            VMEM((DEPTH, SHARD, HALF_LANES), BF),
            VMEM((DEPTH, SHARD, HALF_LANES), BF),
            VMEM((DEPTH, SHARD, HALF_LANES), BF),
            dma((2, len(KEYS))), dma((2, len(KEYS))),
            dma((SEQ,)), dma((SEQ,)),
            dma((2, 8)), dma((2, 8)),
            *pair, *pair,
            dma((2, SEQ)), dma((2, SEQ)),
            dma((2,)), dma((2,)),
            dma((2, DEPTH)), dma((2, DEPTH)),
            dma((DEPTH,)), dma((DEPTH,)),
            dma((CHUNKS,)), dma,
        ],
        compiler_params=pltpu.CompilerParams(
            collective_id=1, has_side_effects=True, vmem_limit_bytes=VMEM_BYTES
        ),
        name="layer",
    )(tokens, w, d_out, rank, index)


def per_device(tokens, w_qkv, vis_index, counts, d_out):
    extra = (counts[0] - SURE).reshape(SIDE, SIDE).T.reshape(SEQ)
    order = jnp.arange(SEQ, dtype=jnp.int32)
    before = jnp.sum(jnp.where(order[None, :] < order[:, None], extra[None, :], 0), axis=1)
    within = jnp.arange(TAIL, dtype=jnp.int32)
    rank = jnp.where(within[None, :] < extra[:, None], before[:, None] + within[None, :], -1)
    rank = rank.reshape(1, SEQ * TAIL).astype(jnp.int32)
    attn_out, d_tokens, d_wqkv = layer_call(tokens, w_qkv.T, d_out, rank, vis_index)
    return attn_out, d_tokens, d_wqkv.T


def solution(mesh):
    placed = (
        P("batch", "seq", None),
        P(None, "seq"),
        P("batch", "seq"),
        P("batch", None),
        P("batch", "seq", None),
    )
    return jax.shard_map(
        per_device,
        mesh=mesh,
        in_specs=placed,
        out_specs=(P("batch", "seq", None), P("batch", "seq", None), P(None, "seq")),
        check_vma=False,
    )
```

```python
import jax
import jax.numpy as jnp
from jax import lax
from jax.experimental import pallas as pl
from jax.experimental.pallas import tpu as pltpu
from jax.sharding import PartitionSpec as P

D = 1408
HEAD = 88
HEADS = 16
CAP = 160
HALF = 80
SURE = 96
TAIL = CAP - SURE
LIVE = 2048
PACKED = LIVE - HEADS * SURE
LANES = 128
WIDE = 3 * LANES
SEQ = 16
SIDE = 4
DEPTH = 8
EPSILON = 1e-06
LOG2E = 1.4426950408889634
LN2 = 0.6931471805599453
SCALE = HEAD ** (-0.5)
MESH = pl.DeviceIdType.MESH
BF = jnp.bfloat16
F32 = jnp.float32
VMEM = pltpu.VMEM
VMEM_BYTES = 62 * 2**20
CHUNKS = 4
CHUNK = 1024 // CHUNKS


def dot(left, right, left_dim=1, right_dim=0):
    return lax.dot_general(
        left, right, (((left_dim,), (right_dim,)), ((), ())), preferred_element_type=F32
    )


def wrap(value, size):
    return lax.rem(value + 2 * size, size)


PART = {0: (0, 80), 1: (0, 48), -1: (48, 32)}
BLOCK = {"o": (0, 0), "m": (-1, 0), "p": (1, 0), "a": (2, 1), "b": (2, -1)}
KEYS = (
    [("P1", s) for s in (1, -1)]
    + [("P1f", s) for s in (1, -1)]
    + [("P2", j, s) for j in "ompab" for s in (1, -1)]
    + [("P2f", j, s) for j in "omp" for s in (1, -1)]
    + [("P2f", "a", 1), ("P2f", "b", -1)]
)
IDS = {key: at for at, key in enumerate(KEYS)}


class Tree:
    def __init__(self, me, way, blocks, send_sem, recv_sem):
        self.y, self.x, self.way = me // SIDE, lax.rem(me, SIDE), way
        self.blocks, self.send_sem, self.recv_sem = blocks, send_sem, recv_sem
        self.memo = {}
        self.slots = {}
        for half in (0, 1):
            for first in range(SIDE):
                for second in range(SIDE):
                    self.slot(half, first, second)

    def node(self, half, first, second):
        key = (half, first % SIDE, second % SIDE)
        if key not in self.memo:
            first, second = first * self.way, second * self.way
            dy, dx = (second, first) if half == 0 else (first, second)
            self.memo[key] = wrap(self.y + dy, SIDE) * SIDE + wrap(self.x + dx, SIDE)
        return self.memo[key]

    def slot(self, half, first, second):
        key = (half, first % SIDE, second % SIDE)
        if key not in self.slots:
            node = self.node(half, first, second)
            self.slots[key] = node if half == 0 else lax.rem(node, SIDE) * SIDE + node // SIDE
        return self.slots[key]

    def describe(self, key):
        kind, sign = key[0], key[-1]
        if kind == "P1":
            return (0, 0), 0, 0, sign
        if kind == "P1f":
            return (-sign, 0), sign, 0, sign
        first, part = BLOCK[key[1]]
        if kind == "P2":
            return (first, 0), part, 1, sign
        return (first, -sign), sign, 1, sign

    def copy(self, half, key, receiver=False):
        (first, second), part, axis, sign = self.describe(key)
        if receiver:
            first, second = (first - sign, second) if axis == 0 else (first, second - sign)
        start, rows = PART[part]
        ref = self.blocks.at[half, self.slot(half, first, second), pl.ds(start, rows)]
        to = self.node(half, sign, 0) if axis == 0 else self.node(half, 0, sign)
        return pltpu.make_async_remote_copy(
            src_ref=ref, dst_ref=ref,
            send_sem=self.send_sem.at[half, IDS[key]], recv_sem=self.recv_sem.at[half, IDS[key]],
            device_id={"seq": to}, device_id_type=MESH,
        )

    def start(self, *key):
        for half in (0, 1):
            self.copy(half, key).start()

    def arrive(self, *key):
        for half in (0, 1):
            self.copy(half, key, True).wait_recv()

    def first(self):
        for s in (1, -1):
            self.start("P1", s)
        for s in (1, -1):
            self.start("P2", "o", s)

    def rest(self, done):
        for s in (1, -1):
            self.arrive("P1", s)
            self.start("P1f", s)
        for s in (1, -1):
            self.start("P2", "m", s)
            self.start("P2", "p", s)
        done([(-1, 0), (1, 0)])
        for s in (1, -1):
            self.arrive("P2", "o", s)
            self.start("P2f", "o", s)
        for s in (1, -1):
            self.arrive("P1f", s)
            for t in (1, -1):
                self.start("P2", "a" if s == 1 else "b", t)
        done([(0, -1), (0, 1), (2, 0)])
        for j in ("m", "p"):
            for s in (1, -1):
                self.arrive("P2", j, s)
                self.start("P2f", j, s)
        done([(-1, -1), (-1, 1), (1, -1), (1, 1)])
        for j in ("a", "b"):
            for s in (1, -1):
                self.arrive("P2", j, s)
                if ("P2f", j, s) in IDS:
                    self.start("P2f", j, s)
        for s in (1, -1):
            self.arrive("P2f", "o", s)
        done([(2, -1), (2, 1), (0, 2)])
        for j in ("m", "p"):
            for s in (1, -1):
                self.arrive("P2f", j, s)
        self.arrive("P2f", "a", 1)
        self.arrive("P2f", "b", -1)
        done([(-1, 2), (1, 2), (2, 2)])

    def finish(self):
        for key in KEYS:
            for half in (0, 1):
                self.copy(half, key).wait_send()


QB = 256


def attend(q, kt, k, va, vat, g, att, dq, dkt, dvt, between):
    dkt[...] = jnp.zeros_like(dkt)
    dvt[...] = jnp.zeros_like(dvt)
    lane = lax.broadcasted_iota(jnp.int32, (QB, LANES), 1)

    def block(at, carry):
        between(at)
        rows = pl.ds(at * QB, QB)
        queries = q[rows]
        scores = dot(queries, kt[...])
        weights = jnp.exp2(scores - jnp.max(scores, axis=1, keepdims=True)).astype(BF)
        raw = dot(weights, va[...])
        inverse = 1.0 / raw[:, HEAD:HEAD + 1]
        out = jnp.where(lane < HEAD, raw * inverse, 0.0)
        att[rows] = out.astype(BF)
        scaled = (g[rows].astype(F32) * inverse).astype(BF)
        delta = jnp.sum(scaled.astype(F32) * out, axis=1, keepdims=True)
        high = delta.astype(BF).astype(F32)
        extended = jnp.where(lane == HEAD, -high, scaled.astype(F32))
        extended = jnp.where(lane == HEAD + 1, high - delta, extended).astype(BF)
        d_scores = weights * dot(extended, vat[...]).astype(BF)
        dq[rows] = (dot(d_scores, k[...]) * SCALE).astype(BF)
        dkt[...] += dot(queries, d_scores, 0, 0)
        dvt[...] += dot(scaled, weights, 0, 0)
        return carry

    lax.fori_loop(0, LIVE // QB, block, 0)


HALF_LANES = 768
SHARD = WIDE // DEPTH
FIRST = SEQ * HALF
MORE = SURE - HALF
PACK_AT = FIRST + SEQ * MORE


def layer_kernel(
    tokens_in, w, d_out, counts, index,
    attn_out, d_rows, d_wqkv,
    rows_buf, blocks, normed_buf, inv_buf, w_side, w3, g_send, g_recv, qkv,
    q, k, v, g, kt, vt, att, dq, dkt, dvt,
    d_send, att_send, att_recv, d_recv, part_send, part_recv,
    turned_d, own_sum, pair_send, pair_recv, z_send, z_recv, z_all, z_other,
    t_ssem, t_rsem, g_ssem, g_rsem, w_ssem, w_rsem,
    d_ssem, d_rsem, p_ssem, p_rsem, a_ssem, a_rsem, c_ssem, c_rsem, z_ssem, z_rsem, o_ssem, o_rsem,
    in_sem,
):
    me = lax.axis_index("seq")
    batch = lax.axis_index("batch")
    core, z = lax.rem(batch, 2), batch // 2
    y, x = me // SIDE, lax.rem(me, SIDE)
    place = (y, x)

    def peer(axis, step):
        if axis == 0:
            return wrap(y + step, SIDE) * SIDE + x
        return y * SIDE + wrap(x + step, SIDE)

    def above(step):
        return wrap(z + step, DEPTH) * 2 + core

    other = batch + 1 - 2 * core

    def fetch(part):
        rows = pl.ds(part * CHUNK, CHUNK)
        return pltpu.make_async_copy(tokens_in.at[0, rows], rows_buf.at[rows], in_sem.at[part])

    for part in range(CHUNKS):
        fetch(part).start()
    barrier = pltpu.get_barrier_semaphore()
    for step in range(1, SEQ):
        pl.semaphore_signal(
            barrier, inc=1, device_id={"seq": lax.rem(me + step, SEQ)}, device_id_type=MESH
        )
    for step in range(1, DEPTH):
        pl.semaphore_signal(
            barrier, inc=1, device_id={"batch": above(step)}, device_id_type=MESH
        )
    pl.semaphore_signal(barrier, inc=1, device_id={"batch": other}, device_id_type=MESH)

    def remote(src, dst, sems, at, to, where="seq"):
        return pltpu.make_async_remote_copy(
            src_ref=src, dst_ref=dst, send_sem=sems[0].at[at], recv_sem=sems[1].at[at],
            device_id={where: to}, device_id_type=MESH,
        )

    g_send[...] = jnp.zeros_like(g_send)
    for head in range(HEADS):
        g_send[head, :, :HEAD] = d_out[0, :, head * HEAD:(head + 1) * HEAD]
    g_sems = (g_ssem, g_rsem)

    def g_copy(step):
        to = lax.rem(me + step, SEQ)
        return remote(g_send.at[to], g_recv.at[me], g_sems, step, to)

    def g_arrival(step):
        origin = lax.rem(me - step + SEQ, SEQ)
        return remote(g_send.at[origin], g_recv.at[origin], g_sems, step, origin)

    def g_start(step, carry):
        g_copy(step).start()
        return carry

    pl.semaphore_wait(barrier, SEQ - 1 + DEPTH)
    lax.fori_loop(1, SEQ, g_start, 0)

    column = jnp.broadcast_to(index[...], (LANES, CAP)).T
    lane = lax.broadcasted_iota(jnp.int32, (CAP, LANES), 1)
    picked = None
    for part in range(CHUNKS):
        hot = jnp.concatenate(
            [
                (column == lane + (part * CHUNK + first)).astype(BF)
                for first in range(0, CHUNK, LANES)
            ],
            axis=1,
        )
        fetch(part).wait()
        rows = dot(hot, rows_buf[part * CHUNK:(part + 1) * CHUNK])
        picked = rows if picked is None else picked + rows
    centred = picked - jnp.mean(picked, axis=1, keepdims=True)
    inv_std = lax.rsqrt(jnp.mean(centred * centred, axis=1, keepdims=True) + EPSILON)
    normed = centred * inv_std
    blocks[0, me] = normed[:HALF].astype(BF)
    blocks[1, x * SIDE + y] = normed[HALF:].astype(BF)
    tree = Tree(me, 1 - 2 * core, blocks, t_ssem, t_rsem)
    tree.first()
    normed_buf[...] = normed
    inv_buf[...] = jnp.broadcast_to(inv_std, inv_buf.shape)

    w_side[:, :, :, SURE:, :] = jnp.zeros((2, SIDE, 3, LANES - SURE, D), BF)
    for axis in (0, 1):
        for part in range(3):
            w_side[axis, place[axis], part, :HEAD] = w[part * HEAD:(part + 1) * HEAD]
            w_side[axis, place[axis], part, HEAD:SURE] = jnp.zeros((SURE - HEAD, D), BF)
    w3[...] = w_side[0, y].reshape(WIDE, D).T
    g_recv[me] = g_send[me]

    lane = lax.broadcasted_iota(jnp.int32, (1, WIDE), 1)
    column_scale = jnp.where(lane < LANES, SCALE * LOG2E, 1.0).astype(F32)

    def project(offsets):
        places = [(half, tree.slot(half, *offset)) for half in (0, 1) for offset in offsets]
        rows = jnp.concatenate([blocks[at] for at in places], axis=0)
        out = (dot(rows, w3[...]) * column_scale).astype(BF)
        for at, (half, slot) in enumerate(places):
            qkv[half, slot] = out[at * HALF:(at + 1) * HALF]

    project([(0, 0)])
    tree.rest(project)

    w_sems = (w_ssem, w_rsem)
    way = 1 - 2 * core
    share = SURE // 2
    PIECE = {0: (0, share), 1: (0, 32), -1: (32, share - 32)}

    def w_part(axis, step, piece, whose):
        start, rows = PIECE[piece]
        start = pl.multiple_of(whose * share + start, 16)
        return w_side.at[axis, wrap(place[axis] + step, SIDE), :, pl.ds(start, rows)]

    def w_move(ref, axis, slot, sign, to, where="seq"):
        return remote(ref, ref, w_sems, (axis, slot + (1 - sign) // 2), to, where)

    def w_own(axis, sign):
        return w_move(w_part(axis, 0, 0, core), axis, 0, sign, peer(axis, sign * way))

    def w_from(axis, sign):
        return w_move(w_part(axis, -sign * way, 0, core), axis, 0, sign, peer(axis, -sign * way))

    def w_onward(axis, sign, hops=1):
        return w_move(w_part(axis, -hops * sign * way, sign, core), axis, 2, sign, peer(axis, sign * way))

    def w_across(axis, sign, far, receiver=False):
        whose, side = (1 - core, -way) if receiver else (core, way)
        step, piece = (-2 * sign * side, sign) if far else (-sign * side, 0)
        return w_move(w_part(axis, step, piece, whose), axis, 6 if far else 4, sign, other, "batch")

    def arrival(ref, sems, axis, step):
        part = ref.at[axis, wrap(place[axis] - step, SIDE)]
        return remote(part, part, sems, (axis, step), peer(axis, step))

    def g_wait(step, carry):
        g_copy(step).wait_send()
        g_arrival(step).wait_recv()
        return carry

    lax.fori_loop(1, SEQ, g_wait, 0)
    for axis in (0, 1):
        for sign in (1, -1):
            w_own(axis, sign).start()
    turned = [column * SIDE + row for row in range(SIDE) for column in range(SIDE)]
    slot = lax.broadcasted_iota(jnp.int32, (1, HEADS * TAIL), 1)
    rank = jnp.full_like(slot, -1)
    before = 0
    for at, owner in enumerate(turned):
        extra = counts[0, owner] - SURE
        within = slot - at * TAIL
        rank = jnp.where((within >= 0) & (within < extra), before + within, rank)
        before = before + extra
    hot = (lax.broadcasted_iota(jnp.int32, (PACKED, HEADS * TAIL), 0) == rank).astype(BF)
    g[:FIRST] = g_recv[:, :HALF, :].reshape(FIRST, LANES)
    for at, owner in enumerate(turned):
        g[FIRST + at * MORE:FIRST + (at + 1) * MORE] = g_recv[owner, HALF:SURE, :]
    g_tail = jnp.concatenate([g_recv[owner, SURE:, :] for owner in turned], axis=0)
    g[PACK_AT:] = dot(hot, g_tail).astype(BF)

    tail = dot(hot, qkv[1, :, MORE:, :].reshape(HEADS * TAIL, WIDE)).astype(BF)
    for part, ref in enumerate((q, k, v)):
        lanes = slice(part * LANES, (part + 1) * LANES)
        ref[:FIRST] = qkv[0, :, :, lanes].reshape(FIRST, LANES)
        ref[FIRST:PACK_AT] = qkv[1, :, :MORE, lanes].reshape(SEQ * MORE, LANES)
        ref[PACK_AT:] = tail[:, lanes]
    lane = lax.broadcasted_iota(jnp.int32, (LIVE, LANES), 1)
    ones = (lane == HEAD) | (lane == HEAD + 1)
    v[...] = jnp.where(ones, 1.0, v[...].astype(F32)).astype(BF)
    kt[...] = k[...].T
    vt[...] = v[...].T

    a_sems = (a_ssem, a_rsem)

    def a_part(ref, half, node):
        return ref.at[node, pl.ds(half * HALF, HALF)]

    def a_copy(half, step):
        to = lax.rem(me + step, SEQ)
        return remote(a_part(att_send, half, to), a_part(att_recv, half, me), a_sems, (half, step), to)

    def a_arrival(half, step):
        origin = lax.rem(me - step + SEQ, SEQ)
        part = a_part(att_recv, half, origin)
        return remote(part, part, a_sems, (half, step), origin)

    def a_start(half):
        def one(step, carry):
            a_copy(half, step).start()
            return carry

        lax.fori_loop(1, SEQ, one, 0)

    def between(at):
        @pl.when(at == 4)
        def _():
            for axis in (0, 1):
                for sign in (1, -1):
                    w_from(axis, sign).wait_recv()
                    w_onward(axis, sign).start()
            for axis in (0, 1):
                for sign in (1, -1):
                    w_across(axis, sign, False).start()

        @pl.when(at == FIRST // QB)
        def _():
            att_send[:, :HALF, :] = att[:FIRST].reshape(SEQ, HALF, LANES)
            a_start(0)

        @pl.when(at == LIVE // QB - 1)
        def _():
            for axis in (0, 1):
                for sign in (1, -1):
                    w_onward(axis, sign, 2).wait_recv()
                    w_across(axis, sign, True).start()

    attend(q, kt, k, v, vt, g, att, dq, dkt, dvt, between)

    dk = (dkt[...].T * LN2).astype(BF)
    dv = dvt[...].T.astype(BF)
    packed = jnp.concatenate([dq[PACK_AT:], dk[PACK_AT:], dv[PACK_AT:], att[PACK_AT:]], axis=1)
    loose = dot(hot, packed, 0, 0).astype(BF).reshape(SIDE, SIDE, TAIL, 4 * LANES)
    for part, value in enumerate((dq, dk, dv)):
        lanes = slice(part * LANES, (part + 1) * LANES)
        d_send[0, :, :, :, lanes] = value[:FIRST].reshape(SIDE, SIDE, HALF, LANES)
        d_send[1, :, :, :MORE, lanes] = value[FIRST:PACK_AT].reshape(SIDE, SIDE, MORE, LANES)
    d_send[1, :, :, MORE:, :] = loose[..., :WIDE]

    d_sems = (d_ssem, d_rsem)

    def d_copy(axis, step):
        to = wrap(place[axis] + step, SIDE)
        return remote(
            d_send.at[axis, to], d_recv.at[axis, place[axis]], d_sems, (axis, step), peer(axis, step)
        )

    for step in (2, 1, 3):
        for axis in (0, 1):
            d_copy(axis, step).start()
    for axis in (0, 1):
        d_recv[axis, place[axis]] = d_send[axis, place[axis]]

    def lanes_of(which):
        return pl.ds(pl.multiple_of(which * (D - HALF_LANES), LANES), HALF_LANES)

    turned_d[...] = d_send[...].reshape(SEQ * CAP, WIDE).T

    def product(which):
        return dot(turned_d[...], blocks[:, :, :, lanes_of(which)].reshape(SEQ * CAP, HALF_LANES))

    pair_send[...] = product(1 - core).astype(BF)
    c_sems = (c_ssem, c_rsem)
    pair_copy = remote(pair_send, pair_recv, c_sems, 0, other, "batch")
    pair_copy.start()
    for at, owner in enumerate(turned):
        att_send[owner, HALF:SURE, :] = att[FIRST + at * MORE:FIRST + (at + 1) * MORE]
        att_send[owner, SURE:, :] = loose[at // SIDE, at % SIDE, :, WIDE:]
    a_start(1)
    att_recv[me] = att_send[me]
    own_sum[...] = product(core)

    z_sems = (z_ssem, z_rsem)

    def z_copy(phase, step):
        src = z_send.at[wrap(z + step, DEPTH)] if phase == 0 else z_all.at[z]
        dst = (z_recv if phase == 0 else z_all).at[z]
        return remote(src, dst, z_sems, (phase, step), above(step), "batch")

    def z_arrival(phase, step):
        ref = (z_recv if phase == 0 else z_all).at[wrap(z - step, DEPTH)]
        return remote(ref, ref, z_sems, (phase, step), above(step), "batch")

    pair_copy.wait()
    z_send[...] = (own_sum[...] + pair_recv[...].astype(F32)).astype(BF).reshape(
        DEPTH, SHARD, HALF_LANES
    )
    for step in (4, 3, 5, 2, 6, 1, 7):
        z_copy(0, step).start()
    z_recv[z] = z_send[z]

    p_sems = (p_ssem, p_rsem)

    def p_copy(axis, step):
        to = wrap(place[axis] + step, SIDE)
        return remote(
            part_send.at[axis, to], part_recv.at[axis, place[axis]], p_sems, (axis, step), peer(axis, step)
        )

    for axis in (0, 1):
        for sign in (1, -1):
            w_across(axis, sign, False, True).wait_recv()
            w_across(axis, sign, True, True).wait_recv()
        for step in (1, 2, 3):
            arrival(d_recv, d_sems, axis, step).wait_recv()
        left = jnp.concatenate(
            [d_recv[axis, head].reshape(SIDE * HALF, WIDE) for head in range(SIDE)], axis=1
        )
        partial = dot(left, w_side[axis].reshape(SIDE * WIDE, D))
        part_send[1 - axis] = partial.astype(BF).reshape(SIDE, HALF, D)
        for step in (2, 1, 3):
            p_copy(1 - axis, step).start()
    for axis in (0, 1):
        part_recv[axis, place[axis]] = part_send[axis, place[axis]]

    def a_wait(step, carry):
        for half in (0, 1):
            a_copy(half, step).wait_send()
            a_arrival(half, step).wait_recv()
        return carry

    lax.fori_loop(1, SEQ, a_wait, 0)
    for head in range(HEADS):
        attn_out[0, :, head * HEAD:(head + 1) * HEAD] = att_recv[head, :, :HEAD]

    for step in range(1, DEPTH):
        z_arrival(0, step).wait_recv()
    total = z_recv[0].astype(F32)
    for at in range(1, DEPTH):
        total = total + z_recv[at].astype(F32)
    z_all[z] = total.astype(BF)
    for step in (4, 3, 5, 2, 6, 1, 7):
        z_copy(1, step).start()

    def o_copy(step):
        slot = wrap(z - step, DEPTH)
        return remote(z_all.at[slot], z_other.at[slot], (o_ssem, o_rsem), step, other, "batch")

    o_copy(0).start()

    for axis in (0, 1):
        for step in (1, 2, 3):
            arrival(part_recv, p_sems, axis, step).wait_recv()
    halves = []
    for axis in (1, 0):
        value = part_recv[axis, 0].astype(F32)
        for at in range(1, SIDE):
            value = value + part_recv[axis, at].astype(F32)
        halves.append(value)
    d_normed = jnp.concatenate(halves, axis=0)
    normed = normed_buf[...]
    d_picked = inv_buf[:, :1] * (
        d_normed
        - jnp.mean(d_normed, axis=1, keepdims=True)
        - normed * jnp.mean(d_normed * normed, axis=1, keepdims=True)
    )
    d_rows[...] = d_picked.astype(BF)

    for step in (1, 7, 2, 6, 3, 5, 4):
        z_arrival(1, step).wait_recv()
        o_copy(step).start()
    for step in range(DEPTH):
        o_copy(step).wait()
    mine, theirs = (
        ref[...].reshape(WIDE, HALF_LANES) for ref in (z_all, z_other)
    )
    low = jnp.where(core == 0, mine, theirs)
    high = jnp.where(core == 0, theirs, mine)
    overlap = 2 * HALF_LANES - D
    for part in range(3):
        rows = slice(part * HEAD, (part + 1) * HEAD)
        padded = slice(part * LANES, part * LANES + HEAD)
        d_wqkv[rows, :HALF_LANES] = low[padded]
        d_wqkv[rows, HALF_LANES:] = high[padded, overlap:]

    for axis in (0, 1):
        for sign in (1, -1):
            w_own(axis, sign).wait_send()
            w_onward(axis, sign).wait_send()
            w_across(axis, sign, False).wait_send()
            w_across(axis, sign, True).wait_send()
        for step in (1, 2, 3):
            d_copy(axis, step).wait_send()
            p_copy(axis, step).wait_send()
    for step in range(1, DEPTH):
        z_copy(0, step).wait_send()
        z_copy(1, step).wait_send()
    tree.finish()


def layer_call(tokens, w, d_out, counts, index):
    vmem = pl.BlockSpec(memory_space=VMEM)
    anywhere = pl.BlockSpec(memory_space=pl.ANY)
    dma = pltpu.SemaphoreType.DMA
    positions = tokens.shape[1]
    pair = [dma((2, SIDE)), dma((2, SIDE))]
    return pl.pallas_call(
        layer_kernel,
        out_shape=(
            jax.ShapeDtypeStruct((1, CAP, D), BF),
            jax.ShapeDtypeStruct((CAP, D), BF),
            jax.ShapeDtypeStruct((3 * HEAD, D), BF),
        ),
        in_specs=[anywhere, vmem, vmem, pl.BlockSpec(memory_space=pltpu.SMEM), vmem],
        out_specs=(vmem,) * 3,
        scratch_shapes=[
            VMEM((positions, D), BF),
            VMEM((2, SEQ, HALF, D), BF),
            VMEM((CAP, D), F32),
            VMEM((CAP, LANES), F32),
            VMEM((2, SIDE, 3, LANES, D), BF),
            VMEM((D, WIDE), BF),
            VMEM((SEQ, CAP, LANES), BF),
            VMEM((SEQ, CAP, LANES), BF),
            VMEM((2, SEQ, HALF, WIDE), BF),
            VMEM((LIVE, LANES), BF),
            VMEM((LIVE, LANES), BF),
            VMEM((LIVE, LANES), BF),
            VMEM((LIVE, LANES), BF),
            VMEM((LANES, LIVE), BF),
            VMEM((LANES, LIVE), BF),
            VMEM((LIVE, LANES), BF),
            VMEM((LIVE, LANES), BF),
            VMEM((LANES, LIVE), F32),
            VMEM((LANES, LIVE), F32),
            VMEM((2, SIDE, SIDE, HALF, WIDE), BF),
            VMEM((SEQ, CAP, LANES), BF),
            VMEM((SEQ, CAP, LANES), BF),
            VMEM((2, SIDE, SIDE, HALF, WIDE), BF),
            VMEM((2, SIDE, HALF, D), BF),
            VMEM((2, SIDE, HALF, D), BF),
            VMEM((WIDE, SEQ * CAP), BF),
            VMEM((WIDE, HALF_LANES), F32),
            VMEM((WIDE, HALF_LANES), BF),
            VMEM((WIDE, HALF_LANES), BF),
            VMEM((DEPTH, SHARD, HALF_LANES), BF),
            VMEM((DEPTH, SHARD, HALF_LANES), BF),
            VMEM((DEPTH, SHARD, HALF_LANES), BF),
            VMEM((DEPTH, SHARD, HALF_LANES), BF),
            dma((2, len(KEYS))), dma((2, len(KEYS))),
            dma((SEQ,)), dma((SEQ,)),
            dma((2, 8)), dma((2, 8)),
            *pair, *pair,
            dma((2, SEQ)), dma((2, SEQ)),
            dma((2,)), dma((2,)),
            dma((2, DEPTH)), dma((2, DEPTH)),
            dma((DEPTH,)), dma((DEPTH,)),
            dma((CHUNKS,)),
        ],
        compiler_params=pltpu.CompilerParams(
            collective_id=1, has_side_effects=True, vmem_limit_bytes=VMEM_BYTES
        ),
        name="layer",
    )(tokens, w, d_out, counts, index)


def finish_kernel(attn, d_rows, d_wqkv, index, attn_out, d_tokens, d_wqkv_out):
    at = pl.program_id(0)

    @pl.when(at == 0)
    def _():
        attn_out[...] = attn[...]
        d_wqkv_out[...] = d_wqkv[...].astype(F32)

    position = lax.broadcasted_iota(jnp.int32, (CHUNK, CAP), 0) + at * CHUNK
    d_tokens[0] = dot((position == index[...]).astype(BF), d_rows[...]).astype(BF)


def finish_call(attn, d_rows, d_wqkv, index, positions):
    def whole(array):
        return pl.BlockSpec(array.shape, lambda at: (0,) * array.ndim)

    return pl.pallas_call(
        finish_kernel,
        grid=(positions // CHUNK,),
        out_shape=(
            jax.ShapeDtypeStruct(attn.shape, BF),
            jax.ShapeDtypeStruct((1, positions, D), BF),
            jax.ShapeDtypeStruct(d_wqkv.shape, F32),
        ),
        in_specs=[whole(attn), whole(d_rows), whole(d_wqkv), whole(index)],
        out_specs=(
            whole(attn),
            pl.BlockSpec((1, CHUNK, D), lambda at: (0, at, 0)),
            whole(d_wqkv),
        ),
        compiler_params=pltpu.CompilerParams(vmem_limit_bytes=32 * 2**20),
        name="finish",
    )(attn, d_rows, d_wqkv, index)


def per_device(tokens, w_qkv, vis_index, counts, d_out):
    attn, d_rows, d_wqkv = layer_call(tokens, w_qkv.T, d_out, counts, vis_index)
    attn_out, d_tokens, d_wqkv = finish_call(attn, d_rows, d_wqkv, vis_index, tokens.shape[1])
    return attn_out, d_tokens, d_wqkv.T


def solution(mesh):
    placed = (
        P("batch", "seq", None),
        P(None, "seq"),
        P("batch", "seq"),
        P("batch", None),
        P("batch", "seq", None),
    )
    return jax.shard_map(
        per_device,
        mesh=mesh,
        in_specs=placed,
        out_specs=(P("batch", "seq", None), P("batch", "seq", None), P(None, "seq")),
        check_vma=False,
    )
```

```python
import jax
import jax.numpy as jnp
from jax import lax
from jax.experimental import pallas as pl
from jax.experimental.pallas import tpu as pltpu
from jax.sharding import PartitionSpec as P

D = 1408
HEAD = 88
HEADS = 16
CAP = 160
HALF = 80
SURE = 96
TAIL = CAP - SURE
LIVE = 2048
PACKED = LIVE - HEADS * SURE
LANES = 128
WIDE = 3 * LANES
SEQ = 16
SIDE = 4
DEPTH = 8
EPSILON = 1e-06
LOG2E = 1.4426950408889634
LN2 = 0.6931471805599453
SCALE = HEAD ** (-0.5)
MESH = pl.DeviceIdType.MESH
BF = jnp.bfloat16
F32 = jnp.float32
VMEM = pltpu.VMEM
VMEM_BYTES = 62 * 2**20
CHUNKS = 4
CHUNK = 1024 // CHUNKS


def dot(left, right, left_dim=1, right_dim=0):
    return lax.dot_general(
        left, right, (((left_dim,), (right_dim,)), ((), ())), preferred_element_type=F32
    )


def wrap(value, size):
    return lax.rem(value + 2 * size, size)


PART = {0: (0, 80), 1: (0, 48), -1: (48, 32)}
BLOCK = {"o": (0, 0), "m": (-1, 0), "p": (1, 0), "a": (2, 1), "b": (2, -1)}
KEYS = (
    [("P1", s) for s in (1, -1)]
    + [("P1f", s) for s in (1, -1)]
    + [("P2", j, s) for j in "ompab" for s in (1, -1)]
    + [("P2f", j, s) for j in "omp" for s in (1, -1)]
    + [("P2f", "a", 1), ("P2f", "b", -1)]
)
IDS = {key: at for at, key in enumerate(KEYS)}


class Tree:
    def __init__(self, me, way, blocks, send_sem, recv_sem):
        self.y, self.x, self.way = me // SIDE, lax.rem(me, SIDE), way
        self.blocks, self.send_sem, self.recv_sem = blocks, send_sem, recv_sem
        self.memo = {}
        self.slots = {}
        for half in (0, 1):
            for first in range(SIDE):
                for second in range(SIDE):
                    self.slot(half, first, second)

    def node(self, half, first, second):
        key = (half, first % SIDE, second % SIDE)
        if key not in self.memo:
            first, second = first * self.way, second * self.way
            dy, dx = (second, first) if half == 0 else (first, second)
            self.memo[key] = wrap(self.y + dy, SIDE) * SIDE + wrap(self.x + dx, SIDE)
        return self.memo[key]

    def slot(self, half, first, second):
        key = (half, first % SIDE, second % SIDE)
        if key not in self.slots:
            node = self.node(half, first, second)
            self.slots[key] = node if half == 0 else lax.rem(node, SIDE) * SIDE + node // SIDE
        return self.slots[key]

    def describe(self, key):
        kind, sign = key[0], key[-1]
        if kind == "P1":
            return (0, 0), 0, 0, sign
        if kind == "P1f":
            return (-sign, 0), sign, 0, sign
        first, part = BLOCK[key[1]]
        if kind == "P2":
            return (first, 0), part, 1, sign
        return (first, -sign), sign, 1, sign

    def copy(self, half, key, receiver=False):
        (first, second), part, axis, sign = self.describe(key)
        if receiver:
            first, second = (first - sign, second) if axis == 0 else (first, second - sign)
        start, rows = PART[part]
        ref = self.blocks.at[half, self.slot(half, first, second), pl.ds(start, rows)]
        to = self.node(half, sign, 0) if axis == 0 else self.node(half, 0, sign)
        return pltpu.make_async_remote_copy(
            src_ref=ref, dst_ref=ref,
            send_sem=self.send_sem.at[half, IDS[key]], recv_sem=self.recv_sem.at[half, IDS[key]],
            device_id={"seq": to}, device_id_type=MESH,
        )

    def start(self, *key):
        for half in (0, 1):
            self.copy(half, key).start()

    def arrive(self, *key):
        for half in (0, 1):
            self.copy(half, key, True).wait_recv()

    def first(self):
        for s in (1, -1):
            self.start("P1", s)
        for s in (1, -1):
            self.start("P2", "o", s)

    def rest(self, done):
        for s in (1, -1):
            self.arrive("P1", s)
            self.start("P1f", s)
        for s in (1, -1):
            self.start("P2", "m", s)
            self.start("P2", "p", s)
        done([(-1, 0), (1, 0)])
        for s in (1, -1):
            self.arrive("P2", "o", s)
            self.start("P2f", "o", s)
        for s in (1, -1):
            self.arrive("P1f", s)
            for t in (1, -1):
                self.start("P2", "a" if s == 1 else "b", t)
        done([(0, -1), (0, 1), (2, 0)])
        for j in ("m", "p"):
            for s in (1, -1):
                self.arrive("P2", j, s)
                self.start("P2f", j, s)
        done([(-1, -1), (-1, 1), (1, -1), (1, 1)])
        for j in ("a", "b"):
            for s in (1, -1):
                self.arrive("P2", j, s)
                if ("P2f", j, s) in IDS:
                    self.start("P2f", j, s)
        for s in (1, -1):
            self.arrive("P2f", "o", s)
        done([(2, -1), (2, 1), (0, 2)])
        for j in ("m", "p"):
            for s in (1, -1):
                self.arrive("P2f", j, s)
        self.arrive("P2f", "a", 1)
        self.arrive("P2f", "b", -1)
        done([(-1, 2), (1, 2), (2, 2)])

    def finish(self):
        for key in KEYS:
            for half in (0, 1):
                self.copy(half, key).wait_send()


QB = 256


def attend(q, kt, k, va, vat, g, att, dq, dkt, dvt, between):
    dkt[...] = jnp.zeros_like(dkt)
    dvt[...] = jnp.zeros_like(dvt)
    lane = lax.broadcasted_iota(jnp.int32, (QB, LANES), 1)

    def block(at, carry):
        between(at)
        rows = pl.ds(at * QB, QB)
        queries = q[rows]
        scores = dot(queries, kt[...])
        weights = jnp.exp2(scores - jnp.max(scores, axis=1, keepdims=True)).astype(BF)
        raw = dot(weights, va[...])
        inverse = 1.0 / raw[:, HEAD:HEAD + 1]
        out = jnp.where(lane < HEAD, raw * inverse, 0.0)
        att[rows] = out.astype(BF)
        scaled = (g[rows].astype(F32) * inverse).astype(BF)
        delta = jnp.sum(scaled.astype(F32) * out, axis=1, keepdims=True)
        high = delta.astype(BF).astype(F32)
        extended = jnp.where(lane == HEAD, -high, scaled.astype(F32))
        extended = jnp.where(lane == HEAD + 1, high - delta, extended).astype(BF)
        d_scores = weights * dot(extended, vat[...]).astype(BF)
        dq[rows] = (dot(d_scores, k[...]) * SCALE).astype(BF)
        dkt[...] += dot(queries, d_scores, 0, 0)
        dvt[...] += dot(scaled, weights, 0, 0)
        return carry

    lax.fori_loop(0, LIVE // QB, block, 0)


HALF_LANES = 768
SHARD = WIDE // DEPTH
FIRST = SEQ * HALF
MORE = SURE - HALF
PACK_AT = FIRST + SEQ * MORE


def layer_kernel(
    tokens_in, w, d_out, counts, index,
    attn_out, d_rows, d_wqkv,
    rows_buf, blocks, normed_buf, inv_buf, w_side, w3, g_send, g_recv, qkv,
    q, k, v, g, kt, vt, att, dq, dkt, dvt,
    d_send, att_send, att_recv, d_recv, part_send, part_recv,
    turned_d, own_sum, pair_send, pair_recv, z_send, z_recv, z_all, z_other,
    t_ssem, t_rsem, g_ssem, g_rsem, w_ssem, w_rsem,
    d_ssem, d_rsem, p_ssem, p_rsem, a_ssem, a_rsem, c_ssem, c_rsem, z_ssem, z_rsem, o_ssem, o_rsem,
    in_sem,
):
    me = lax.axis_index("seq")
    batch = lax.axis_index("batch")
    core, z = lax.rem(batch, 2), batch // 2
    y, x = me // SIDE, lax.rem(me, SIDE)
    place = (y, x)

    def peer(axis, step):
        if axis == 0:
            return wrap(y + step, SIDE) * SIDE + x
        return y * SIDE + wrap(x + step, SIDE)

    def above(step):
        return wrap(z + step, DEPTH) * 2 + core

    other = batch + 1 - 2 * core

    def fetch(part):
        rows = pl.ds(part * CHUNK, CHUNK)
        return pltpu.make_async_copy(tokens_in.at[0, rows], rows_buf.at[rows], in_sem.at[part])

    for part in range(CHUNKS):
        fetch(part).start()
    barrier = pltpu.get_barrier_semaphore()
    for step in range(1, SEQ):
        pl.semaphore_signal(
            barrier, inc=1, device_id={"seq": lax.rem(me + step, SEQ)}, device_id_type=MESH
        )
    for step in range(1, DEPTH):
        pl.semaphore_signal(
            barrier, inc=1, device_id={"batch": above(step)}, device_id_type=MESH
        )
    pl.semaphore_signal(barrier, inc=1, device_id={"batch": other}, device_id_type=MESH)

    def remote(src, dst, sems, at, to, where="seq"):
        return pltpu.make_async_remote_copy(
            src_ref=src, dst_ref=dst, send_sem=sems[0].at[at], recv_sem=sems[1].at[at],
            device_id={where: to}, device_id_type=MESH,
        )

    g_send[...] = jnp.zeros_like(g_send)
    for head in range(HEADS):
        g_send[head, :, :HEAD] = d_out[0, :, head * HEAD:(head + 1) * HEAD]
    g_sems = (g_ssem, g_rsem)

    def g_copy(step):
        to = lax.rem(me + step, SEQ)
        return remote(g_send.at[to], g_recv.at[me], g_sems, step, to)

    def g_arrival(step):
        origin = lax.rem(me - step + SEQ, SEQ)
        return remote(g_send.at[origin], g_recv.at[origin], g_sems, step, origin)

    def g_start(step, carry):
        g_copy(step).start()
        return carry

    pl.semaphore_wait(barrier, SEQ - 1 + DEPTH)
    lax.fori_loop(1, SEQ, g_start, 0)

    column = jnp.broadcast_to(index[...], (LANES, CAP)).T
    lane = lax.broadcasted_iota(jnp.int32, (CAP, LANES), 1)
    picked = None
    for part in range(CHUNKS):
        hot = jnp.concatenate(
            [
                (column == lane + (part * CHUNK + first)).astype(BF)
                for first in range(0, CHUNK, LANES)
            ],
            axis=1,
        )
        fetch(part).wait()
        rows = dot(hot, rows_buf[part * CHUNK:(part + 1) * CHUNK])
        picked = rows if picked is None else picked + rows
    centred = picked - jnp.mean(picked, axis=1, keepdims=True)
    inv_std = lax.rsqrt(jnp.mean(centred * centred, axis=1, keepdims=True) + EPSILON)
    normed = centred * inv_std
    blocks[0, me] = normed[:HALF].astype(BF)
    blocks[1, x * SIDE + y] = normed[HALF:].astype(BF)
    tree = Tree(me, 1 - 2 * core, blocks, t_ssem, t_rsem)
    tree.first()
    normed_buf[...] = normed
    inv_buf[...] = jnp.broadcast_to(inv_std, inv_buf.shape)

    w_side[:, :, :, SURE:, :] = jnp.zeros((2, SIDE, 3, LANES - SURE, D), BF)
    for axis in (0, 1):
        for part in range(3):
            w_side[axis, place[axis], part, :HEAD] = w[part * HEAD:(part + 1) * HEAD]
            w_side[axis, place[axis], part, HEAD:SURE] = jnp.zeros((SURE - HEAD, D), BF)
    w3[...] = w_side[0, y].reshape(WIDE, D).T
    g_recv[me] = g_send[me]

    lane = lax.broadcasted_iota(jnp.int32, (1, WIDE), 1)
    column_scale = jnp.where(lane < LANES, SCALE * LOG2E, 1.0).astype(F32)

    def project(offsets):
        places = [(half, tree.slot(half, *offset)) for half in (0, 1) for offset in offsets]
        rows = jnp.concatenate([blocks[at] for at in places], axis=0)
        out = (dot(rows, w3[...]) * column_scale).astype(BF)
        for at, (half, slot) in enumerate(places):
            qkv[half, slot] = out[at * HALF:(at + 1) * HALF]

    project([(0, 0)])
    tree.rest(project)

    w_sems = (w_ssem, w_rsem)
    way = 1 - 2 * core
    share = SURE // 2
    PIECE = {0: (0, share), 1: (0, 32), -1: (32, share - 32)}

    def w_part(axis, step, piece, whose):
        start, rows = PIECE[piece]
        start = pl.multiple_of(whose * share + start, 16)
        return w_side.at[axis, wrap(place[axis] + step, SIDE), :, pl.ds(start, rows)]

    def w_move(ref, axis, slot, sign, to, where="seq"):
        return remote(ref, ref, w_sems, (axis, slot + (1 - sign) // 2), to, where)

    def w_own(axis, sign):
        return w_move(w_part(axis, 0, 0, core), axis, 0, sign, peer(axis, sign * way))

    def w_from(axis, sign):
        return w_move(w_part(axis, -sign * way, 0, core), axis, 0, sign, peer(axis, -sign * way))

    def w_onward(axis, sign, hops=1):
        return w_move(w_part(axis, -hops * sign * way, sign, core), axis, 2, sign, peer(axis, sign * way))

    def w_across(axis, sign, far, receiver=False):
        whose, side = (1 - core, -way) if receiver else (core, way)
        step, piece = (-2 * sign * side, sign) if far else (-sign * side, 0)
        return w_move(w_part(axis, step, piece, whose), axis, 6 if far else 4, sign, other, "batch")

    def arrival(ref, sems, axis, step):
        part = ref.at[axis, wrap(place[axis] - step, SIDE)]
        return remote(part, part, sems, (axis, step), peer(axis, step))

    def g_wait(step, carry):
        g_copy(step).wait_send()
        g_arrival(step).wait_recv()
        return carry

    lax.fori_loop(1, SEQ, g_wait, 0)
    for axis in (0, 1):
        for sign in (1, -1):
            w_own(axis, sign).start()
    turned = [column * SIDE + row for row in range(SIDE) for column in range(SIDE)]
    slot = lax.broadcasted_iota(jnp.int32, (1, HEADS * TAIL), 1)
    rank = jnp.full_like(slot, -1)
    before = 0
    for at, owner in enumerate(turned):
        extra = counts[0, owner] - SURE
        within = slot - at * TAIL
        rank = jnp.where((within >= 0) & (within < extra), before + within, rank)
        before = before + extra
    hot = (lax.broadcasted_iota(jnp.int32, (PACKED, HEADS * TAIL), 0) == rank).astype(BF)
    g[:FIRST] = g_recv[:, :HALF, :].reshape(FIRST, LANES)
    for at, owner in enumerate(turned):
        g[FIRST + at * MORE:FIRST + (at + 1) * MORE] = g_recv[owner, HALF:SURE, :]
    g_tail = jnp.concatenate([g_recv[owner, SURE:, :] for owner in turned], axis=0)
    g[PACK_AT:] = dot(hot, g_tail).astype(BF)

    tail = dot(hot, qkv[1, :, MORE:, :].reshape(HEADS * TAIL, WIDE)).astype(BF)
    for part, ref in enumerate((q, k, v)):
        lanes = slice(part * LANES, (part + 1) * LANES)
        ref[:FIRST] = qkv[0, :, :, lanes].reshape(FIRST, LANES)
        ref[FIRST:PACK_AT] = qkv[1, :, :MORE, lanes].reshape(SEQ * MORE, LANES)
        ref[PACK_AT:] = tail[:, lanes]
    lane = lax.broadcasted_iota(jnp.int32, (LIVE, LANES), 1)
    ones = (lane == HEAD) | (lane == HEAD + 1)
    v[...] = jnp.where(ones, 1.0, v[...].astype(F32)).astype(BF)
    kt[...] = k[...].T
    vt[...] = v[...].T

    a_sems = (a_ssem, a_rsem)

    def a_part(ref, half, node):
        return ref.at[node, pl.ds(half * HALF, HALF)]

    def a_copy(half, step):
        to = lax.rem(me + step, SEQ)
        return remote(a_part(att_send, half, to), a_part(att_recv, half, me), a_sems, (half, step), to)

    def a_arrival(half, step):
        origin = lax.rem(me - step + SEQ, SEQ)
        part = a_part(att_recv, half, origin)
        return remote(part, part, a_sems, (half, step), origin)

    def a_start(half):
        def one(step, carry):
            a_copy(half, step).start()
            return carry

        lax.fori_loop(1, SEQ, one, 0)

    def between(at):
        @pl.when(at == 4)
        def _():
            for axis in (0, 1):
                for sign in (1, -1):
                    w_from(axis, sign).wait_recv()
                    w_onward(axis, sign).start()
            for axis in (0, 1):
                for sign in (1, -1):
                    w_across(axis, sign, False).start()

        @pl.when(at == FIRST // QB)
        def _():
            att_send[:, :HALF, :] = att[:FIRST].reshape(SEQ, HALF, LANES)
            a_start(0)

    attend(q, kt, k, v, vt, g, att, dq, dkt, dvt, between)

    dk = (dkt[...].T * LN2).astype(BF)
    dv = dvt[...].T.astype(BF)
    packed = jnp.concatenate([dq[PACK_AT:], dk[PACK_AT:], dv[PACK_AT:], att[PACK_AT:]], axis=1)
    loose = dot(hot, packed, 0, 0).astype(BF).reshape(SIDE, SIDE, TAIL, 4 * LANES)
    for part, value in enumerate((dq, dk, dv)):
        lanes = slice(part * LANES, (part + 1) * LANES)
        d_send[0, :, :, :, lanes] = value[:FIRST].reshape(SIDE, SIDE, HALF, LANES)
        d_send[1, :, :, :MORE, lanes] = value[FIRST:PACK_AT].reshape(SIDE, SIDE, MORE, LANES)
    d_send[1, :, :, MORE:, :] = loose[..., :WIDE]

    d_sems = (d_ssem, d_rsem)

    def d_copy(axis, step):
        to = wrap(place[axis] + step, SIDE)
        return remote(
            d_send.at[axis, to], d_recv.at[axis, place[axis]], d_sems, (axis, step), peer(axis, step)
        )

    for step in (2, 1, 3):
        for axis in (0, 1):
            d_copy(axis, step).start()
    for axis in (0, 1):
        for sign in (1, -1):
            w_onward(axis, sign, 2).wait_recv()
            w_across(axis, sign, True).start()
    for axis in (0, 1):
        d_recv[axis, place[axis]] = d_send[axis, place[axis]]

    def lanes_of(which):
        return pl.ds(pl.multiple_of(which * (D - HALF_LANES), LANES), HALF_LANES)

    turned_d[...] = d_send[...].reshape(SEQ * CAP, WIDE).T

    def product(which):
        return dot(turned_d[...], blocks[:, :, :, lanes_of(which)].reshape(SEQ * CAP, HALF_LANES))

    pair_send[...] = product(1 - core).astype(BF)
    c_sems = (c_ssem, c_rsem)
    pair_copy = remote(pair_send, pair_recv, c_sems, 0, other, "batch")
    pair_copy.start()
    for at, owner in enumerate(turned):
        att_send[owner, HALF:SURE, :] = att[FIRST + at * MORE:FIRST + (at + 1) * MORE]
        att_send[owner, SURE:, :] = loose[at // SIDE, at % SIDE, :, WIDE:]
    a_start(1)
    att_recv[me] = att_send[me]
    own_sum[...] = product(core)

    z_sems = (z_ssem, z_rsem)

    def z_copy(phase, step):
        src = z_send.at[wrap(z + step, DEPTH)] if phase == 0 else z_all.at[z]
        dst = (z_recv if phase == 0 else z_all).at[z]
        return remote(src, dst, z_sems, (phase, step), above(step), "batch")

    def z_arrival(phase, step):
        ref = (z_recv if phase == 0 else z_all).at[wrap(z - step, DEPTH)]
        return remote(ref, ref, z_sems, (phase, step), above(step), "batch")

    pair_copy.wait()
    z_send[...] = (own_sum[...] + pair_recv[...].astype(F32)).astype(BF).reshape(
        DEPTH, SHARD, HALF_LANES
    )
    for step in (4, 3, 5, 2, 6, 1, 7):
        z_copy(0, step).start()
    z_recv[z] = z_send[z]

    p_sems = (p_ssem, p_rsem)

    def p_copy(axis, step):
        to = wrap(place[axis] + step, SIDE)
        return remote(
            part_send.at[axis, to], part_recv.at[axis, place[axis]], p_sems, (axis, step), peer(axis, step)
        )

    for axis in (0, 1):
        for sign in (1, -1):
            w_across(axis, sign, False, True).wait_recv()
            w_across(axis, sign, True, True).wait_recv()
        for step in (1, 2, 3):
            arrival(d_recv, d_sems, axis, step).wait_recv()
        left = jnp.concatenate(
            [d_recv[axis, head].reshape(SIDE * HALF, WIDE) for head in range(SIDE)], axis=1
        )
        partial = dot(left, w_side[axis].reshape(SIDE * WIDE, D))
        part_send[1 - axis] = partial.astype(BF).reshape(SIDE, HALF, D)
        for step in (2, 1, 3):
            p_copy(1 - axis, step).start()
    for axis in (0, 1):
        part_recv[axis, place[axis]] = part_send[axis, place[axis]]

    for step in range(1, DEPTH):
        z_arrival(0, step).wait_recv()
    total = z_recv[0].astype(F32)
    for at in range(1, DEPTH):
        total = total + z_recv[at].astype(F32)
    z_all[z] = total.astype(BF)
    for step in (4, 3, 5, 2, 6, 1, 7):
        z_copy(1, step).start()

    def o_copy(step):
        slot = wrap(z - step, DEPTH)
        return remote(z_all.at[slot], z_other.at[slot], (o_ssem, o_rsem), step, other, "batch")

    o_copy(0).start()

    def a_wait(step, carry):
        for half in (0, 1):
            a_copy(half, step).wait_send()
            a_arrival(half, step).wait_recv()
        return carry

    lax.fori_loop(1, SEQ, a_wait, 0)
    for head in range(HEADS):
        attn_out[0, :, head * HEAD:(head + 1) * HEAD] = att_recv[head, :, :HEAD]

    for axis in (0, 1):
        for step in (1, 2, 3):
            arrival(part_recv, p_sems, axis, step).wait_recv()
    halves = []
    for axis in (1, 0):
        value = part_recv[axis, 0].astype(F32)
        for at in range(1, SIDE):
            value = value + part_recv[axis, at].astype(F32)
        halves.append(value)
    d_normed = jnp.concatenate(halves, axis=0)
    normed = normed_buf[...]
    d_picked = inv_buf[:, :1] * (
        d_normed
        - jnp.mean(d_normed, axis=1, keepdims=True)
        - normed * jnp.mean(d_normed * normed, axis=1, keepdims=True)
    )
    d_rows[...] = d_picked.astype(BF)

    for step in (1, 7, 2, 6, 3, 5, 4):
        z_arrival(1, step).wait_recv()
        o_copy(step).start()
    for step in range(DEPTH):
        o_copy(step).wait()
    mine, theirs = (
        ref[...].reshape(WIDE, HALF_LANES) for ref in (z_all, z_other)
    )
    low = jnp.where(core == 0, mine, theirs)
    high = jnp.where(core == 0, theirs, mine)
    overlap = 2 * HALF_LANES - D
    for part in range(3):
        rows = slice(part * HEAD, (part + 1) * HEAD)
        padded = slice(part * LANES, part * LANES + HEAD)
        d_wqkv[rows, :HALF_LANES] = low[padded]
        d_wqkv[rows, HALF_LANES:] = high[padded, overlap:]

    for axis in (0, 1):
        for sign in (1, -1):
            w_own(axis, sign).wait_send()
            w_onward(axis, sign).wait_send()
            w_across(axis, sign, False).wait_send()
            w_across(axis, sign, True).wait_send()
        for step in (1, 2, 3):
            d_copy(axis, step).wait_send()
            p_copy(axis, step).wait_send()
    for step in range(1, DEPTH):
        z_copy(0, step).wait_send()
        z_copy(1, step).wait_send()
    tree.finish()


def layer_call(tokens, w, d_out, counts, index):
    vmem = pl.BlockSpec(memory_space=VMEM)
    anywhere = pl.BlockSpec(memory_space=pl.ANY)
    dma = pltpu.SemaphoreType.DMA
    positions = tokens.shape[1]
    pair = [dma((2, SIDE)), dma((2, SIDE))]
    return pl.pallas_call(
        layer_kernel,
        out_shape=(
            jax.ShapeDtypeStruct((1, CAP, D), BF),
            jax.ShapeDtypeStruct((CAP, D), BF),
            jax.ShapeDtypeStruct((3 * HEAD, D), BF),
        ),
        in_specs=[anywhere, vmem, vmem, pl.BlockSpec(memory_space=pltpu.SMEM), vmem],
        out_specs=(vmem,) * 3,
        scratch_shapes=[
            VMEM((positions, D), BF),
            VMEM((2, SEQ, HALF, D), BF),
            VMEM((CAP, D), F32),
            VMEM((CAP, LANES), F32),
            VMEM((2, SIDE, 3, LANES, D), BF),
            VMEM((D, WIDE), BF),
            VMEM((SEQ, CAP, LANES), BF),
            VMEM((SEQ, CAP, LANES), BF),
            VMEM((2, SEQ, HALF, WIDE), BF),
            VMEM((LIVE, LANES), BF),
            VMEM((LIVE, LANES), BF),
            VMEM((LIVE, LANES), BF),
            VMEM((LIVE, LANES), BF),
            VMEM((LANES, LIVE), BF),
            VMEM((LANES, LIVE), BF),
            VMEM((LIVE, LANES), BF),
            VMEM((LIVE, LANES), BF),
            VMEM((LANES, LIVE), F32),
            VMEM((LANES, LIVE), F32),
            VMEM((2, SIDE, SIDE, HALF, WIDE), BF),
            VMEM((SEQ, CAP, LANES), BF),
            VMEM((SEQ, CAP, LANES), BF),
            VMEM((2, SIDE, SIDE, HALF, WIDE), BF),
            VMEM((2, SIDE, HALF, D), BF),
            VMEM((2, SIDE, HALF, D), BF),
            VMEM((WIDE, SEQ * CAP), BF),
            VMEM((WIDE, HALF_LANES), F32),
            VMEM((WIDE, HALF_LANES), BF),
            VMEM((WIDE, HALF_LANES), BF),
            VMEM((DEPTH, SHARD, HALF_LANES), BF),
            VMEM((DEPTH, SHARD, HALF_LANES), BF),
            VMEM((DEPTH, SHARD, HALF_LANES), BF),
            VMEM((DEPTH, SHARD, HALF_LANES), BF),
            dma((2, len(KEYS))), dma((2, len(KEYS))),
            dma((SEQ,)), dma((SEQ,)),
            dma((2, 8)), dma((2, 8)),
            *pair, *pair,
            dma((2, SEQ)), dma((2, SEQ)),
            dma((2,)), dma((2,)),
            dma((2, DEPTH)), dma((2, DEPTH)),
            dma((DEPTH,)), dma((DEPTH,)),
            dma((CHUNKS,)),
        ],
        compiler_params=pltpu.CompilerParams(
            collective_id=1, has_side_effects=True, vmem_limit_bytes=VMEM_BYTES
        ),
        name="layer",
    )(tokens, w, d_out, counts, index)


def finish_kernel(attn, d_rows, d_wqkv, index, attn_out, d_tokens, d_wqkv_out):
    at = pl.program_id(0)

    @pl.when(at == 0)
    def _():
        attn_out[...] = attn[...]
        d_wqkv_out[...] = d_wqkv[...].astype(F32)

    position = lax.broadcasted_iota(jnp.int32, (CHUNK, CAP), 0) + at * CHUNK
    d_tokens[0] = dot((position == index[...]).astype(BF), d_rows[...]).astype(BF)


def finish_call(attn, d_rows, d_wqkv, index, positions):
    def whole(array):
        return pl.BlockSpec(array.shape, lambda at: (0,) * array.ndim)

    return pl.pallas_call(
        finish_kernel,
        grid=(positions // CHUNK,),
        out_shape=(
            jax.ShapeDtypeStruct(attn.shape, BF),
            jax.ShapeDtypeStruct((1, positions, D), BF),
            jax.ShapeDtypeStruct(d_wqkv.shape, F32),
        ),
        in_specs=[whole(attn), whole(d_rows), whole(d_wqkv), whole(index)],
        out_specs=(
            whole(attn),
            pl.BlockSpec((1, CHUNK, D), lambda at: (0, at, 0)),
            whole(d_wqkv),
        ),
        compiler_params=pltpu.CompilerParams(vmem_limit_bytes=VMEM_BYTES),
        name="finish",
    )(attn, d_rows, d_wqkv, index)


def per_device(tokens, w_qkv, vis_index, counts, d_out):
    attn, d_rows, d_wqkv = layer_call(tokens, w_qkv.T, d_out, counts, vis_index)
    attn_out, d_tokens, d_wqkv = finish_call(attn, d_rows, d_wqkv, vis_index, tokens.shape[1])
    return attn_out, d_tokens, d_wqkv.T


def solution(mesh):
    placed = (
        P("batch", "seq", None),
        P(None, "seq"),
        P("batch", "seq"),
        P("batch", None),
        P("batch", "seq", None),
    )
    return jax.shard_map(
        per_device,
        mesh=mesh,
        in_specs=placed,
        out_specs=(P("batch", "seq", None), P("batch", "seq", None), P(None, "seq")),
        check_vma=False,
    )
```
